32 devices in a mesh: groups: 2 (over y), row: 4 (over z), col: 4 (over x, core).
Axes of the slice: x: 2, y: 2, z: 4, core: 2. Of those that a mesh axis runs over, the one named last changes fastest.
Arguments:
- factor_blocks: bfloat16 [20, 4096, 4096], P('groups', 'row', 'col'), parts along dimension 0, may hold values from -0.0390625 to 0.0390625
- inverse_blocks: bfloat16 [10, 4096, 4096], P('groups', 'col', 'row'), parts along dimension 0, as said below
- right_sides: bfloat16 [10, 4096, 256], P('groups', 'row'), parts along dimension 0, may hold values from -6 to 6
Outputs:
- solution: bfloat16 [10, 4096, 256], P('groups', 'col', 'row'), parts along dimension 0
The draws below stay inside these ranges and needn't reach their ends.
There are 2 independent parts, one for each index of `groups`. The reference program is written for one: setup_inputs(seed, part) draws one part's arguments, and reference() takes and returns one part's arrays. A program takes and returns all parts, laid end to end along the dimension named above; each array names one. Nothing has to cross between parts.
Inputs may be any that keep to these rules, and one draw needn't show every extreme that they name: `inverse_blocks`: each block is lower triangular with a diagonal of 0.5 to 2, hence invertible.
All inputs are finite; a program needn't handle non-finite values.
Results may differ from the reference program's by a relative error of at most 0.0095.
Values may be sent and summed in bfloat16 or wider, within the bound.
No kernel may reach another device: no remote copies, remote signals or barrier semaphores. Data moves between devices by JAX's collectives and lax.ppermute only.
A program may use at most 64 MiB of HBM per device.

```python
import jax
import jax.numpy as jnp
from jax import lax

BS = 4096
NB = 5
R = 256
ORDER = 20480
NPAIR = 10
N_ROW = 4


def draw_inverse_blocks(key, part):
    base = jax.random.fold_in(key, 4177)
    key_diag, key_off = jax.random.split(base, 2)
    diagonal = jnp.exp(jax.random.uniform(key_diag, (NB, BS), jnp.float32, jnp.log(0.5), jnp.log(2.0)))
    lower = jax.random.normal(key_off, (NB, BS, BS), jnp.float32) * (0.6 / jnp.sqrt(BS * 1.0))
    rows = jnp.arange(BS)[:, None]
    cols = jnp.arange(BS)[None, :]
    strict = (rows > cols).astype(jnp.float32)
    eye = (rows == cols).astype(jnp.float32)
    whole = diagonal[:, :, None] * eye[None] + lower * strict[None]
    return whole.astype(jnp.bfloat16)


def block_levels(stream_key, extent, shards, smallest, largest):
    def one(position, parts):
        draws = jax.random.uniform(jax.random.fold_in(jax.random.fold_in(stream_key, 6), position), (parts,), jnp.float32, smallest / len(shards), largest / len(shards))
        return jnp.repeat(jnp.exp(draws), extent[position] // parts).reshape((-1,) + (1,) * (len(extent) - position - 1))

    level = one(*shards[0])
    for cut in shards[1:]:
        level = level * one(*cut)
    return level


def normal_values(rng, dims, scale, reach, cuts=(), kind=jnp.bfloat16):
    result = jax.random.normal(rng, dims, jnp.float32) * scale
    if len(cuts) > 0:
        result = block_levels(rng, dims, cuts, -0.22, 0.18) * result
    return jnp.clip(result, min=-reach, max=reach).astype(kind)


def setup_inputs(seed: int = 0, part: int = 0) -> dict:
    seeds = jax.random.split(jax.random.key(seed), 4)
    part_splits = jax.random.split(jax.random.fold_in(seeds[3], part), 4)
    return {
        "factor_blocks": normal_values(part_splits[0], (NPAIR, BS, BS), ORDER ** -0.5, 0.0390625, ((1, 4), (2, 4))),
        "inverse_blocks": draw_inverse_blocks(jax.random.fold_in(jax.random.fold_in(seeds[3], part), 71), part),
        "right_sides": normal_values(part_splits[2], (NB, BS, R), 1.0, 6.0, ((1, 4),)),
    }


def pair_index(block_row, column_index):
    return block_row * (block_row - 1) // 2 + column_index


def reference(factor_blocks, inverse_blocks, right_sides):
    solved = []
    group_rows = BS // N_ROW
    for block_row in range(NB):
        residual = right_sides[block_row].astype(jnp.float32)
        if block_row > 0:
            strip = jnp.concatenate([factor_blocks[pair_index(block_row, j)] for j in range(block_row)], axis=1)
            known = jnp.concatenate(solved, axis=0)
            residual = residual - jnp.dot(strip, known, preferred_element_type=jnp.float32)
        residual_bf = residual.astype(jnp.bfloat16)
        inverse = inverse_blocks[block_row].astype(jnp.float32).reshape(BS, N_ROW, group_rows)
        grouped = residual_bf.astype(jnp.float32).reshape(N_ROW, group_rows, R)
        terms = jnp.einsum("iqk,qkr->qir", inverse, grouped, precision=lax.Precision.HIGHEST)
        solved.append(jnp.sum(terms, axis=0).astype(jnp.bfloat16))
    return jnp.stack(solved, axis=0)
```

```python
import jax
import jax.numpy as jnp
from jax import lax
from jax.sharding import PartitionSpec as P

STREAMS = 2


def pair_index(block_row, column_index):
    return block_row * (block_row - 1) // 2 + column_index


def times_transposed(left, right):
    return lax.dot_general(left, right, (((1,), (1,)), ((), ())), preferred_element_type=jnp.float32)


def entry(stacked, index):
    return lax.dynamic_index_in_dim(stacked, index, 0, keepdims=False)


def make_per_device(n_row, n_col):
    siblings = [(c, c ^ 1) for c in range(n_col)]

    def swap(value):
        return lax.ppermute(value, "col", siblings)

    def col_sum(own):
        step = 2
        while step < n_col:
            arrived = lax.ppermute(own.astype(jnp.bfloat16), "col", [(c, c ^ step) for c in range(n_col)])
            own = own + arrived.astype(jnp.float32)
            step *= 2
        return own

    def row_reduce_scatter(parts, place):
        total = entry(parts, place)
        arrived = []
        for shift in range(1, n_row):
            leaving = entry(parts, (place + shift) % n_row).astype(jnp.bfloat16)
            arrived.append(lax.ppermute(leaving, "row", [(i, (i + shift) % n_row) for i in range(n_row)]))
        for value in arrived:
            total = total + value.astype(jnp.float32)
        return total

    def row_all_gather(share, place):
        held = [share]
        for shift in range(n_row - 1, 0, -1):
            held.append(lax.ppermute(share, "row", [(i, (i + shift) % n_row) for i in range(n_row)]))
        twice = jnp.stack(held + held, axis=0)
        return lax.dynamic_slice_in_dim(twice, (n_row - place) % n_row, n_row, 0)

    def per_device(factor_blocks, inverse_blocks, right_sides):
        steps_total, group_rows, angles = right_sides.shape
        col_rows = inverse_blocks.shape[1]
        place = lax.axis_index("row")
        core = lax.axis_index("col") % 2
        half = angles // 2
        wide = half // STREAMS
        pieces = 2 * col_rows // n_row
        sides = jnp.swapaxes(right_sides, 1, 2).reshape(steps_total, 2, half, group_rows)
        sides = jnp.where(core == 0, sides, sides[:, ::-1])
        inverse_twin = swap(inverse_blocks)
        factor_twin = [None] + [swap(factor_blocks[pair_index(i, i - 1)]) for i in range(1, steps_total)]

        def solve_rest(terms):
            parts = jnp.swapaxes(terms.reshape(2, wide, n_row // 2, pieces), 1, 2)
            share = row_reduce_scatter(parts.reshape(n_row, wide, pieces), place).astype(jnp.bfloat16)
            whole = row_all_gather(share, place).reshape(2, n_row // 2, wide, pieces)
            return jnp.swapaxes(whole, 1, 2).reshape(2, wide, col_rows)

        outputs = []
        complete = []
        solved = None
        for step in range(steps_total):
            if step == 0:
                first = times_transposed(sides[0].reshape(angles, group_rows), inverse_blocks[0])
                first = first.reshape(2, half, col_rows)
                arrived = swap(first[1].astype(jnp.bfloat16)).astype(jnp.float32)
                terms = [
                    jnp.stack([first[0, s * wide : (s + 1) * wide], arrived[s * wide : (s + 1) * wide]])
                    for s in range(STREAMS)
                ]
            else:
                older = None
                if step > 1:
                    older = sum(
                        times_transposed(
                            complete[j].reshape(angles, col_rows), factor_blocks[pair_index(step, j)]
                        )
                        for j in range(step - 1)
                    ).reshape(2, half, group_rows)
                    older = older[0] + swap(older[1].astype(jnp.bfloat16)).astype(jnp.float32)
                terms = []
                for s in range(STREAMS):
                    partial = times_transposed(solved[s][0], factor_blocks[pair_index(step, step - 1)])
                    partial = partial + times_transposed(solved[s][1], factor_twin[step])
                    if older is not None:
                        partial = partial + older[s * wide : (s + 1) * wide]
                    residual = sides[step, 0, s * wide : (s + 1) * wide].astype(jnp.float32)
                    residual = (residual - col_sum(partial)).astype(jnp.bfloat16)
                    terms.append(
                        jnp.stack(
                            [
                                times_transposed(residual, inverse_blocks[step]),
                                times_transposed(residual, inverse_twin[step]),
                            ]
                        )
                    )
            solved = [solve_rest(term) for term in terms]
            every = jnp.concatenate(solved, axis=1)
            complete.append(jnp.stack([every[0], swap(every[1])]))
            ordered = jnp.where(core == 0, complete[step], complete[step][::-1]).reshape(angles, col_rows)
            slot = angles // n_row
            outputs.append(lax.dynamic_slice_in_dim(ordered, place * slot, slot, 0).T)
        return jnp.stack(outputs, axis=0)

    return per_device


def solution(mesh):
    placed = (P("groups", "row", "col"), P("groups", "col", "row"), P("groups", "row", None))
    return jax.shard_map(
        make_per_device(mesh.shape["row"], mesh.shape["col"]),
        mesh=mesh,
        in_specs=placed,
        out_specs=P("groups", "col", "row"),
        check_vma=False,
    )
```

```python
import jax
import jax.numpy as jnp
from jax import lax
from jax.sharding import PartitionSpec as P

STREAMS = 2


def pair_index(block_row, column_index):
    return block_row * (block_row - 1) // 2 + column_index


def times_transposed(left, right):
    return lax.dot_general(left, right, (((1,), (1,)), ((), ())), preferred_element_type=jnp.float32)


def make_per_device(n_row, n_col):
    def trade(value, axis, step):
        size = n_row if axis == "row" else n_col
        return lax.ppermute(value.astype(jnp.bfloat16), axis, [(i, i ^ step) for i in range(size)])

    def far_sum(value, axis):
        step = 2
        size = n_row if axis == "row" else n_col
        while step < size:
            value = value + trade(value, axis, step).astype(jnp.float32)
            step *= 2
        return value

    def per_device(factor_blocks, inverse_blocks, right_sides):
        steps_total, group_rows, angles = right_sides.shape
        place = lax.axis_index("row")
        core = lax.axis_index("col")
        side = (place ^ core) & 1
        units = 2 * STREAMS
        wide = angles // units

        def ordered(step):
            cut = right_sides[step].T.reshape(STREAMS, 2, wide, group_rows)
            return jnp.where(side == 0, cut, cut[:, ::-1])

        solved = []
        outputs = []
        for step in range(steps_total):
            base = ordered(step)
            current = []
            for s in range(STREAMS):
                if step == 0:
                    own, other = base[s, 0], base[s, 1]
                else:
                    before = [solved[j][s] for j in range(step)]
                    shares = []
                    for unit in (1, 0):
                        share = times_transposed(before[-1][unit], factor_blocks[pair_index(step, step - 1)])
                        for j in range(step - 1):
                            share = share + times_transposed(before[j][unit], factor_blocks[pair_index(step, j)])
                        shares.append(share)
                    share = shares[1] + trade(shares[0], "col", 1).astype(jnp.float32)
                    share = far_sum(share, "col")
                    own = (base[s, 0].astype(jnp.float32) - share).astype(jnp.bfloat16)
                    other = trade(own, "col", 1)
                term_other = times_transposed(other, inverse_blocks[step])
                term_own = times_transposed(own, inverse_blocks[step])
                total = term_own + trade(term_other, "row", 1).astype(jnp.float32)
                mine = far_sum(total, "row").astype(jnp.bfloat16)
                current.append((mine, trade(mine, "row", 1)))
            solved.append(current)
            slot = angles // n_row
            unit = place * units // n_row
            found = current[0][0]
            for s in range(STREAMS):
                for u in range(2):
                    found = jnp.where(unit == 2 * s + (u ^ side), current[s][u], found)
            within = (place % (n_row // units)) * slot if n_row > units else 0
            outputs.append(lax.dynamic_slice_in_dim(found, within, slot, 0).T)
        return jnp.stack(outputs, axis=0)

    return per_device


def solution(mesh):
    placed = (P("groups", "row", "col"), P("groups", "col", "row"), P("groups", "row", None))
    return jax.shard_map(
        make_per_device(mesh.shape["row"], mesh.shape["col"]),
        mesh=mesh,
        in_specs=placed,
        out_specs=P("groups", "col", "row"),
        check_vma=False,
    )
```

```python
import jax
import jax.numpy as jnp
from jax import lax
from jax.sharding import PartitionSpec as P

STREAMS = 2
UNITS = 2 * STREAMS


def pair_index(block_row, column_index):
    return block_row * (block_row - 1) // 2 + column_index


def times_transposed(left, right):
    return lax.dot_general(left, right, (((1,), (1,)), ((), ())), preferred_element_type=jnp.float32)


def wide(value):
    return value.astype(jnp.float32)


def narrow(value):
    return value.astype(jnp.bfloat16)


class Order:
    def __init__(self):
        self.last = None

    def run(self, work, *values):
        if self.last is not None:
            *values, _ = lax.optimization_barrier((*values, self.last))
        result = work(*values)
        self.last = result[0] if isinstance(result, tuple) else result
        return result


def make_per_device(n_row, n_col):
    def trade(value, axis, step):
        size = n_row if axis == "row" else n_col
        return lax.ppermute(value, axis, [(i, i ^ step) for i in range(size)])

    def more_rounds(value, axis):
        size = n_row if axis == "row" else n_col
        step = 4
        while step < size:
            value = value + wide(trade(narrow(value), axis, step))
            step *= 2
        return value

    def per_device(factor_blocks, inverse_blocks, right_sides):
        steps_total, group_rows, angles = right_sides.shape
        last_step = steps_total - 1
        place = lax.axis_index("row")
        core = lax.axis_index("col") & 1
        side = (place & 1) ^ core
        width = angles // UNITS
        exact = n_row == UNITS
        order = Order()

        def sides_of(step):
            def work(cut):
                cut = cut.T.reshape(STREAMS, 2, width, group_rows)
                return jnp.where(side == 0, cut, cut[:, ::-1])

            return order.run(work, right_sides[step])

        base = [None] * steps_total
        solved = [[None] * STREAMS for _ in range(steps_total)]
        state = [dict() for _ in range(STREAMS)]

        def factor(step, before):
            return factor_blocks[pair_index(step, before)]

        def older(s, step):
            if step >= steps_total or step < 2:
                return
            state[s]["next"] = order.run(
                lambda *known: sum(times_transposed(x, factor(step, j)) for j, x in enumerate(known)),
                *[jnp.concatenate(solved[j][s], axis=0) for j in range(step - 1)],
            )

        def factor_own(s, step):
            st = state[s]
            st["older"] = st.pop("next", None)

            def work(x, *rest):
                value = times_transposed(x, factor(step, step - 1))
                return value + rest[0] if rest else value

            rest = [] if st["older"] is None else [st["older"][:width]]
            st["sum"] = order.run(work, solved[step - 1][s][0], *rest)

        def factor_other(s, step):
            st = state[s]

            def work(x, *rest):
                value = times_transposed(x, factor(step, step - 1))
                return narrow(value + rest[0] if rest else value)

            rest = [] if st["older"] is None else [st["older"][width:]]
            st["flight"] = trade(order.run(work, solved[step - 1][s][1], *rest), "col", 1)

        def chip_sum(s):
            st = state[s]

            def work(value, arrived):
                value = value + wide(arrived)
                return narrow(value), value

            leaving, st["sum"] = order.run(work, st["sum"], st["flight"])
            st["flight"] = trade(leaving, "col", 2) if n_col > 2 else None

        def residual(s, step):
            st = state[s]

            def work(side_values, value, *arrived):
                for a in arrived:
                    value = more_rounds(value + wide(a), "col")
                return narrow(wide(side_values) - value)

            arrived = [] if st["flight"] is None else [st["flight"]]
            st["own"] = order.run(work, base[step][s, 0], st["sum"], *arrived)
            st["flight"] = trade(st["own"], "col", 1)

        def inverse_own(s, step):
            st = state[s]
            st["total"] = order.run(lambda x: times_transposed(x, inverse_blocks[step]), st["own"])

        def inverse_other(s, step):
            st = state[s]
            leaving = order.run(lambda x: narrow(times_transposed(x, inverse_blocks[step])), st["flight"])
            st["flight"] = trade(leaving, "row", 1)

        def pair_sum(s):
            st = state[s]

            def work(value, arrived):
                value = value + wide(arrived)
                return narrow(value), value

            st["leaving"], st["total"] = order.run(work, st["total"], st["flight"])

        def cross(s):
            st = state[s]
            st["flight"] = trade(st["leaving"], "row", 2) if n_row > 2 else None

        def solve(s, step):
            st = state[s]

            def work(value, *arrived):
                for a in arrived:
                    value = more_rounds(value + wide(a), "row")
                return narrow(value)

            arrived = [] if st["flight"] is None else [st["flight"]]
            own = order.run(work, st["total"], *arrived)
            solved[step][s] = (own, trade(own, "row", 1))

        def final_inverse(s):
            st = state[s]

            def leave(own, other):
                return narrow(times_transposed(jnp.where(core == 0, other, own), inverse_blocks[last_step]))

            def keep(own, other):
                return times_transposed(jnp.where(core == 0, own, other), inverse_blocks[last_step])

            leaving = order.run(leave, st["own"], st["flight"])
            st["total"] = order.run(keep, st["own"], st["flight"])
            st["flight"] = trade(leaving, "row", 1)

        base[0] = sides_of(0)
        leaving = order.run(
            lambda x: narrow(times_transposed(x, inverse_blocks[0])),
            base[0][:, 1].reshape(STREAMS * width, group_rows),
        )
        state[0]["flight"] = trade(leaving[:width], "row", 1)
        totals = order.run(
            lambda x: times_transposed(x, inverse_blocks[0]),
            base[0][:, 0].reshape(STREAMS * width, group_rows),
        )
        state[0]["total"], state[1]["total"] = totals[:width], totals[width:]
        pair_sum(0)
        cross(0)
        state[1]["flight"] = trade(order.run(lambda x: x, leaving[width:]), "row", 1)
        if steps_total > 1:
            base[1] = sides_of(1)
        solve(0, 0)
        if steps_total > 1:
            factor_own(0, 1)

        for step in range(1, steps_total):
            final = exact and step == last_step
            factor_other(0, step)
            pair_sum(1)
            cross(1)
            chip_sum(0)
            older(0, step + 1)
            residual(0, step)
            if not final:
                inverse_own(0, step)
            solve(1, step - 1)
            if final:
                final_inverse(0)
            else:
                inverse_other(0, step)
            factor_own(1, step)
            if step < last_step:
                base[step + 1] = sides_of(step + 1)
            factor_other(1, step)
            pair_sum(0)
            if not final:
                cross(0)
            chip_sum(1)
            older(1, step + 1)
            residual(1, step)
            if not final:
                inverse_own(1, step)
                solve(0, step)
                inverse_other(1, step)
            else:
                final_inverse(1)
            if step < last_step:
                factor_own(0, step + 1)

        pair_sum(1)
        outputs = []
        for step in range(steps_total):
            if exact and step == last_step:
                low = place < n_row // 2
                leaving = order.run(
                    lambda a, b: jnp.where(low, b, a), state[0]["leaving"], state[1]["leaving"]
                )
                arrived = trade(leaving, "row", 2)
                found = narrow(jnp.where(low, state[0]["total"], state[1]["total"]) + wide(arrived))
                outputs.append(found.T)
                continue
            if step == last_step:
                cross(1)
                solve(1, step)
            unit = place * UNITS // n_row
            found = solved[step][0][0]
            for s in range(STREAMS):
                for u in range(2):
                    found = jnp.where(unit == 2 * s + (u ^ side), solved[step][s][u], found)
            if not exact:
                slot = angles // n_row
                found = lax.dynamic_slice_in_dim(found, (place * slot) % width, slot, 0)
            outputs.append(found.T)
        return jnp.stack(outputs, axis=0)

    return per_device


def solution(mesh):
    placed = (P("groups", "row", "col"), P("groups", "col", "row"), P("groups", "row", None))
    return jax.shard_map(
        make_per_device(mesh.shape["row"], mesh.shape["col"]),
        mesh=mesh,
        in_specs=placed,
        out_specs=P("groups", "col", "row"),
        check_vma=False,
    )
```

```python
import functools

import jax
import jax.numpy as jnp
from jax import lax
from jax.experimental import pallas as pl
from jax.experimental.pallas import tpu as pltpu
from jax.sharding import PartitionSpec as P

STREAMS = 2
UNITS = 2 * STREAMS


def pair_index(block_row, column_index):
    return block_row * (block_row - 1) // 2 + column_index


HBM = pl.BlockSpec(memory_space=pltpu.HBM)
VMEM = pl.BlockSpec(memory_space=pltpu.VMEM)
SMEM = pl.BlockSpec(memory_space=pltpu.SMEM)
TILE = 256


def params():
    return pltpu.CompilerParams(vmem_limit_bytes=16 * 2**20)


COST = pl.CostEstimate(flops=1, bytes_accessed=1, transcendentals=0)


def fetch(source, indices, held, sems):
    rows = held.shape[1]
    tile = min(rows, TILE)
    copies = []
    for slot, index in enumerate(indices):
        tiles = []
        for t in range(rows // tile):
            cut = pl.ds(t * tile, tile)
            copy = pltpu.make_async_copy(source.at[index, cut], held.at[slot, cut], sems.at[slot, t])
            copy.start()
            tiles.append((cut, copy))
        copies.append(tiles)
    return copies


def times_transposed(left, right):
    return lax.dot_general(left, right, (((1,), (1,)), ((), ())), preferred_element_type=jnp.float32)


def fetch_scratch(blocks, rows, depth):
    return [
        pltpu.VMEM((blocks, rows, depth), jnp.bfloat16),
        pltpu.SemaphoreType.DMA((blocks, rows // min(rows, TILE))),
    ]


def pair_kernel(index, source, own, other, *refs):
    *older, keep, leave, held, sems = refs
    width = own.shape[0]
    (tiles,) = fetch(source, [index], held, sems)
    x = jnp.concatenate([own[...], other[...]], axis=0)
    for cut, copy in tiles:
        copy.wait()
        value = times_transposed(x, held[0, cut])
        if older:
            value = value + older[0][:, cut]
        keep[:, cut] = value[:width]
        leave[:, cut] = value[width:].astype(jnp.bfloat16)


def pair_product(source, index, own, other, older=None):
    rows, depth = source.shape[1:]
    width = own.shape[0]
    extra = [] if older is None else [older]
    return pl.pallas_call(
        functools.partial(pair_kernel, index),
        out_shape=(
            jax.ShapeDtypeStruct((width, rows), jnp.float32),
            jax.ShapeDtypeStruct((width, rows), jnp.bfloat16),
        ),
        in_specs=[HBM] + [VMEM] * (2 + len(extra)),
        out_specs=(VMEM, VMEM),
        scratch_shapes=fetch_scratch(1, rows, depth),
        compiler_params=params(),
        cost_estimate=COST,
    )(source, own, other, *extra)


def older_kernel(indices, streams, source, *refs):
    out, held, sems = refs[-3:]
    known = refs[: 2 * streams * len(indices)]
    before = refs[2 * streams * len(indices) : -3]
    copies = fetch(source, indices, held, sems)
    for slot, tiles in enumerate(copies):
        units = known[2 * streams * slot : 2 * streams * (slot + 1)]
        x = jnp.concatenate([u[...] for u in units], axis=0)
        for cut, copy in tiles:
            copy.wait()
            value = times_transposed(x, held[slot, cut])
            if slot:
                value = value + out[:, cut]
            elif before:
                value = value + before[0][:, cut]
            out[:, cut] = value


def older_products(source, indices, known, before=None):
    rows, depth = source.shape[1:]
    angles = len(known[0]) * known[0][0].shape[0]
    extra = [] if before is None else [before]
    flat = [u for units in known for u in units]
    return pl.pallas_call(
        functools.partial(older_kernel, indices, STREAMS),
        out_shape=jax.ShapeDtypeStruct((angles, rows), jnp.float32),
        in_specs=[HBM] + [VMEM] * (len(flat) + len(extra)),
        out_specs=VMEM,
        scratch_shapes=fetch_scratch(len(indices), rows, depth),
        compiler_params=params(),
        cost_estimate=COST,
    )(source, *flat, *extra)


def first_kernel(s, side, sides, source, keep, leave, product, right, held, sems, right_sem):
    width = keep.shape[0]
    (tiles,) = fetch(source, [0], held, sems)
    copy = pltpu.make_async_copy(sides.at[0, :, pl.ds(2 * s * width, 2 * width)], right, right_sem)
    copy.start()
    copy.wait()
    x = right[...].T
    for cut, tile in tiles:
        tile.wait()
        product[:, cut] = times_transposed(x, held[0, cut])
    own = pl.multiple_of(side[0] * width, width)
    other = pl.multiple_of((1 - side[0]) * width, width)
    keep[...] = product[pl.ds(own, width)]
    leave[...] = product[pl.ds(other, width)].astype(jnp.bfloat16)


def first_products(s, side, sides, source):
    rows, depth = source.shape[1:]
    width = sides.shape[2] // UNITS
    return pl.pallas_call(
        functools.partial(first_kernel, s),
        out_shape=(
            jax.ShapeDtypeStruct((width, rows), jnp.float32),
            jax.ShapeDtypeStruct((width, rows), jnp.bfloat16),
        ),
        in_specs=[SMEM, HBM, HBM],
        out_specs=(VMEM, VMEM),
        scratch_shapes=[
            pltpu.VMEM((2 * width, rows), jnp.float32),
            pltpu.VMEM((depth, 2 * width), jnp.bfloat16),
            *fetch_scratch(1, rows, depth),
            pltpu.SemaphoreType.DMA,
        ],
        compiler_params=params(),
        cost_estimate=COST,
    )(side, sides, source)


def turn_kernel(width, side, sides, out, turned):
    turned[...] = sides[0].T
    for s in range(STREAMS):
        own = pl.multiple_of((2 * s + side[0]) * width, width)
        out[0, s] = turned[pl.ds(own, width)]


def turned_sides(side, sides):
    steps, rows, angles = sides.shape
    width = angles // UNITS
    return pl.pallas_call(
        functools.partial(turn_kernel, width),
        grid=(steps - 1,),
        out_shape=jax.ShapeDtypeStruct((steps - 1, STREAMS, width, rows), jnp.bfloat16),
        in_specs=[SMEM, pl.BlockSpec((1, rows, angles), lambda i: (i + 1, 0, 0))],
        out_specs=pl.BlockSpec((1, STREAMS, width, rows), lambda i: (i, 0, 0, 0)),
        scratch_shapes=[pltpu.VMEM((angles, rows), jnp.bfloat16)],
        compiler_params=params(),
        cost_estimate=COST,
    )(side, sides)


def wide(value):
    return value.astype(jnp.float32)


def narrow(value):
    return value.astype(jnp.bfloat16)


class Order:
    def __init__(self):
        self.last = None

    def run(self, work, *values):
        if self.last is not None:
            *values, _ = lax.optimization_barrier((*values, self.last))
        result = work(*values)
        self.last = result[0] if isinstance(result, (tuple, list)) else result
        return result


def make_per_device(n_row, n_col):
    def trade(value, axis, step):
        size = n_row if axis == "row" else n_col
        return lax.ppermute(value, axis, [(i, i ^ step) for i in range(size)])

    def more_rounds(value, axis):
        size = n_row if axis == "row" else n_col
        step = 4
        while step < size:
            value = value + wide(trade(narrow(value), axis, step))
            step *= 2
        return value

    def per_device(factor_blocks, inverse_blocks, right_sides):
        steps_total, group_rows, angles = right_sides.shape
        last_step = steps_total - 1
        place = lax.axis_index("row")
        core = lax.axis_index("col") & 1
        side = (place & 1) ^ core
        width = angles // UNITS
        exact = n_row == UNITS
        order = Order()

        side_ref = side.astype(jnp.int32).reshape(1)
        solved = [[None] * STREAMS for _ in range(steps_total)]
        state = [dict() for _ in range(STREAMS)]
        sums = [None] * (steps_total + 1)

        def older(step, blocks):
            if step >= steps_total or not blocks:
                return
            units = [[u for s in range(STREAMS) for u in solved[j][s]] for j in blocks]
            flat = [u for known in units for u in known]
            extra = [] if sums[step] is None else [sums[step]]

            def work(*values):
                known = [values[2 * STREAMS * i : 2 * STREAMS * (i + 1)] for i in range(len(blocks))]
                return older_products(
                    factor_blocks, [pair_index(step, j) for j in blocks], known, *values[len(flat) :]
                )

            sums[step] = order.run(work, *flat, *extra)

        def factor(s, step):
            st = state[s]
            rest = [] if sums[step] is None else [sums[step][2 * s * width : 2 * (s + 1) * width]]
            st["sum"], leaving = order.run(
                lambda *v: pair_product(factor_blocks, pair_index(step, step - 1), *v),
                *solved[step - 1][s],
                *rest,
            )
            st["flight"] = trade(leaving, "col", 1)

        def chip_sum(s):
            st = state[s]

            def work(value, arrived):
                value = value + wide(arrived)
                return narrow(value), value

            leaving, st["sum"] = order.run(work, st["sum"], st["flight"])
            st["flight"] = trade(leaving, "col", 2) if n_col > 2 else None

        def residual(s, step):
            st = state[s]

            def work(side_values, value, *arrived):
                for a in arrived:
                    value = more_rounds(value + wide(a), "col")
                return narrow(wide(side_values) - value)

            arrived = [] if st["flight"] is None else [st["flight"]]
            st["own"] = order.run(work, base[step - 1, s], st["sum"], *arrived)
            st["flight"] = trade(st["own"], "col", 1)

        def inverse(s, step):
            st = state[s]
            st["total"], leaving = order.run(
                lambda *v: pair_product(inverse_blocks, step, *v), st["own"], st["flight"]
            )
            st["flight"] = trade(leaving, "row", 1)

        def final_inverse(s):
            st = state[s]
            own, other = st["own"], st["flight"]
            st["own"] = jnp.where(core == 0, own, other)
            st["flight"] = jnp.where(core == 0, other, own)
            inverse(s, last_step)

        def pair_sum(s):
            st = state[s]

            def work(value, arrived):
                value = value + wide(arrived)
                return narrow(value), value

            st["leaving"], st["total"] = order.run(work, st["total"], st["flight"])

        def cross(s):
            st = state[s]
            st["flight"] = trade(st["leaving"], "row", 2) if n_row > 2 else None

        def solve(s, step):
            st = state[s]

            def work(value, *arrived):
                for a in arrived:
                    value = more_rounds(value + wide(a), "row")
                return narrow(value)

            arrived = [] if st["flight"] is None else [st["flight"]]
            own = order.run(work, st["total"], *arrived)
            solved[step][s] = (own, trade(own, "row", 1))

        for s in range(STREAMS):
            state[s]["total"], leaving = order.run(
                lambda v: first_products(s, side_ref, v, inverse_blocks), right_sides
            )
            state[s]["flight"] = trade(leaving, "row", 1)
        if steps_total > 1:
            base = order.run(lambda v: turned_sides(side_ref, v), right_sides)
        for s in range(STREAMS):
            pair_sum(s)
            cross(s)
        solve(0, 0)

        for step in range(1, steps_total):
            final = exact and step == last_step
            factor(0, step)
            if step > 1:
                pair_sum(1)
                cross(1)
            chip_sum(0)
            if step == 1:
                solve(1, 0)
            older(step + 1, range(step - 1))
            residual(0, step)
            if step > 1:
                solve(1, step - 1)
            if final:
                final_inverse(0)
            else:
                inverse(0, step)
            factor(1, step)
            pair_sum(0)
            if not final:
                cross(0)
            chip_sum(1)
            older(step + 1, [step - 1])
            residual(1, step)
            if final:
                final_inverse(1)
            else:
                solve(0, step)
                inverse(1, step)

        pair_sum(1)
        outputs = []
        for step in range(steps_total):
            if exact and step == last_step:
                low = place < n_row // 2
                leaving = order.run(
                    lambda a, b: jnp.where(low, b, a), state[0]["leaving"], state[1]["leaving"]
                )
                arrived = trade(leaving, "row", 2)
                found = narrow(jnp.where(low, state[0]["total"], state[1]["total"]) + wide(arrived))
                outputs.append(found.T)
                continue
            if step == last_step:
                cross(1)
                solve(1, step)
            unit = place * UNITS // n_row
            found = solved[step][0][0]
            for s in range(STREAMS):
                for u in range(2):
                    found = jnp.where(unit == 2 * s + (u ^ side), solved[step][s][u], found)
            if not exact:
                slot = angles // n_row
                found = lax.dynamic_slice_in_dim(found, (place * slot) % width, slot, 0)
            outputs.append(found.T)
        return jnp.stack(outputs, axis=0)

    return per_device


def solution(mesh):
    placed = (P("groups", "row", "col"), P("groups", "col", "row"), P("groups", "row", None))
    return jax.shard_map(
        make_per_device(mesh.shape["row"], mesh.shape["col"]),
        mesh=mesh,
        in_specs=placed,
        out_specs=P("groups", "col", "row"),
        check_vma=False,
    )
```

```python
import functools

import jax
import jax.numpy as jnp
from jax import lax
from jax.experimental import pallas as pl
from jax.experimental.pallas import tpu as pltpu
from jax.sharding import PartitionSpec as P

STREAMS = 2
UNITS = 2 * STREAMS


def pair_index(block_row, column_index):
    return block_row * (block_row - 1) // 2 + column_index


VMEM = pl.BlockSpec(memory_space=pltpu.VMEM)
SMEM = pl.BlockSpec(memory_space=pltpu.SMEM)
COST = pl.CostEstimate(flops=1, bytes_accessed=1, transcendentals=0)


def params():
    return pltpu.CompilerParams(vmem_limit_bytes=16 * 2**20)


def times_transposed(left, right):
    return lax.dot_general(left, right, (((1,), (1,)), ((), ())), preferred_element_type=jnp.float32)


TILE = 256


def product_kernel(count, block, *refs):
    units, rest, out = refs[:count], refs[count:-1], refs[-1]
    x = units[0][...] if count == 1 else jnp.concatenate([u[...] for u in units], axis=0)
    rows = block.shape[0]
    tile = min(rows, TILE)
    for t in range(rows // tile):
        cut = pl.ds(t * tile, tile)
        value = times_transposed(block[cut], x).T
        for r in rest:
            value = value + r[:, cut]
        out[:, cut] = value.astype(out.dtype)


def product(block, units, rest=(), kind=jnp.float32):
    angles = sum(u.shape[0] for u in units)
    return pl.pallas_call(
        functools.partial(product_kernel, len(units)),
        out_shape=jax.ShapeDtypeStruct((angles, block.shape[0]), kind),
        in_specs=[VMEM] * (1 + len(units) + len(rest)),
        out_specs=VMEM,
        compiler_params=params(),
        cost_estimate=COST,
    )(block, *units, *rest)


def first_kernel(s, side, right, block, keep, leave, product):
    width = keep.shape[0]
    x = right[:, pl.ds(2 * s * width, 2 * width)].T
    product[...] = times_transposed(x, block[...])
    own = pl.multiple_of(side[0] * width, width)
    other = pl.multiple_of((1 - side[0]) * width, width)
    leave[...] = product[pl.ds(own, width)].astype(jnp.bfloat16)
    keep[...] = product[pl.ds(other, width)]


def first_products(s, side, right, block):
    rows = block.shape[0]
    width = right.shape[1] // UNITS
    return pl.pallas_call(
        functools.partial(first_kernel, s),
        out_shape=(
            jax.ShapeDtypeStruct((width, rows), jnp.float32),
            jax.ShapeDtypeStruct((width, rows), jnp.bfloat16),
        ),
        in_specs=[SMEM, VMEM, VMEM],
        out_specs=(VMEM, VMEM),
        scratch_shapes=[pltpu.VMEM((2 * width, rows), jnp.float32)],
        compiler_params=params(),
        cost_estimate=COST,
    )(side, right, block)


def turn_kernel(width, side, sides, out, turned):
    turned[...] = sides[0].T
    for s in range(STREAMS):
        own = pl.multiple_of((2 * s + side[0]) * width, width)
        out[0, s] = turned[pl.ds(own, width)]


def turned_sides(side, sides):
    steps, rows, angles = sides.shape
    width = angles // UNITS
    return pl.pallas_call(
        functools.partial(turn_kernel, width),
        grid=(steps - 1,),
        out_shape=jax.ShapeDtypeStruct((steps - 1, STREAMS, width, rows), jnp.bfloat16),
        in_specs=[SMEM, pl.BlockSpec((1, rows, angles), lambda i: (i + 1, 0, 0))],
        out_specs=pl.BlockSpec((1, STREAMS, width, rows), lambda i: (i, 0, 0, 0)),
        scratch_shapes=[pltpu.VMEM((angles, rows), jnp.bfloat16)],
        compiler_params=params(),
        cost_estimate=COST,
    )(side, sides)


def wide(value):
    return value.astype(jnp.float32)


def narrow(value):
    return value.astype(jnp.bfloat16)


class Order:
    def __init__(self):
        self.last = None

    def run(self, work, *values):
        if self.last is not None:
            *values, _ = lax.optimization_barrier((*values, self.last))
        result = work(*values)
        self.last = result[0] if isinstance(result, (tuple, list)) else result
        return result

    def block(self, blocks, index):
        self.last = lax.optimization_barrier(self.run(lambda v: v[index], blocks))
        return self.last


def make_per_device(n_row, n_col):
    def trade(value, axis, step):
        size = n_row if axis == "row" else n_col
        return lax.ppermute(value, axis, [(i, i ^ step) for i in range(size)])

    def more_rounds(value, axis):
        size = n_row if axis == "row" else n_col
        step = 4
        while step < size:
            value = value + wide(trade(narrow(value), axis, step))
            step *= 2
        return value

    def per_device(factor_blocks, inverse_blocks, right_sides):
        steps_total, group_rows, angles = right_sides.shape
        last_step = steps_total - 1
        place = lax.axis_index("row")
        core = lax.axis_index("col") & 1
        side = (place & 1) ^ core
        side_ref = side.astype(jnp.int32).reshape(1)
        width = angles // UNITS
        exact = n_row == UNITS
        order = Order()
        solved = [[None] * STREAMS for _ in range(steps_total)]
        state = [dict() for _ in range(STREAMS)]
        sums = [None] * (steps_total + 1)
        factors = [None] * steps_total
        inverses = [None] * steps_total

        def load_factor(step):
            if step < steps_total:
                factors[step] = order.block(factor_blocks, pair_index(step, step - 1))

        def load_inverse(step):
            if step < steps_total:
                inverses[step] = order.block(inverse_blocks, step)

        def older(step, blocks):
            if step >= steps_total:
                return
            for j in blocks:
                block = order.block(factor_blocks, pair_index(step, j))
                units = [u for s in range(STREAMS) for u in solved[j][s]]

                rest = [] if sums[step] is None else [sums[step]]
                sums[step] = order.run(
                    lambda block, *v: product(block, v[: len(units)], v[len(units) :]), block, *units, *rest
                )

        def older_part(s, step, u):
            first = (2 * s + u) * width
            return [] if sums[step] is None else [sums[step][first : first + width]]

        def factor_other(s, step):
            st = state[s]
            leaving = order.run(
                lambda block, x, *rest: product(block, [x], rest, jnp.bfloat16),
                factors[step],
                solved[step - 1][s][1],
                *older_part(s, step, 1),
            )
            st["swap"] = trade(leaving, "col", 1)

        def factor_own(s, step):
            state[s]["sum"] = order.run(
                lambda block, x, *rest: product(block, [x], rest),
                factors[step],
                solved[step - 1][s][0],
                *older_part(s, step, 0),
            )

        def chip_sum(s):
            def work(value, arrived):
                value = value + wide(arrived)
                return narrow(value), value

            st = state[s]
            leaving, st["sum"] = order.run(work, st["sum"], st["swap"])
            st["flight"] = trade(leaving, "col", 2) if n_col > 2 else None

        def residual(s, step):
            def work(side_values, value, *arrived):
                for a in arrived:
                    value = more_rounds(value + wide(a), "col")
                return narrow(wide(side_values) - value)

            st = state[s]
            arrived = [] if st["flight"] is None else [st["flight"]]
            st["own"] = order.run(work, base[step - 1, s], st["sum"], *arrived)
            st["swap"] = trade(st["own"], "col", 1)

        def inverse_own(s, step):
            st = state[s]
            if exact and step == last_step:
                own, other = st["own"], st["swap"]
                st["own"], st["swap"] = jnp.where(core == 0, other, own), jnp.where(core == 0, own, other)
            leaving = order.run(
                lambda block, x: product(block, [x], kind=jnp.bfloat16), inverses[step], st["own"]
            )
            st["flight"] = trade(leaving, "row", 1)

        def inverse_other(s, step):
            st = state[s]
            st["total"] = order.run(lambda block, x: product(block, [x]), inverses[step], st["swap"])

        def pair_sum(s):
            def work(value, arrived):
                value = value + wide(arrived)
                return narrow(value), value

            st = state[s]
            st["leaving"], st["total"] = order.run(work, st["total"], st["flight"])

        def cross(s):
            st = state[s]
            st["flight"] = trade(st["leaving"], "row", 2) if n_row > 2 else None

        def solve(s, step):
            def work(value, *arrived):
                for a in arrived:
                    value = more_rounds(value + wide(a), "row")
                return narrow(value)

            st = state[s]
            arrived = [] if st["flight"] is None else [st["flight"]]
            other = order.run(work, st["total"], *arrived)
            solved[step][s] = (trade(other, "row", 1), other)

        inverses[0] = order.block(inverse_blocks, 0)
        right = order.block(right_sides, 0)
        for s in range(STREAMS):
            state[s]["total"], leaving = order.run(
                lambda v, w: first_products(s, side_ref, v, w), right, inverses[0]
            )
            state[s]["flight"] = trade(leaving, "row", 1)
        if steps_total > 1:
            base = order.run(lambda v: turned_sides(side_ref, v), right_sides)
        for s in range(STREAMS):
            pair_sum(s)
            cross(s)
        load_factor(1)
        load_inverse(1)

        for step in range(1, steps_total):
            for s in range(STREAMS):
                solve(s, step - 1)
                factor_other(s, step)
            factor_own(0, step)
            chip_sum(0)
            older(step + 1, range(step - 1))
            factor_own(1, step)
            chip_sum(1)
            for s in range(STREAMS):
                residual(s, step)
                inverse_own(s, step)
            for s in range(STREAMS):
                inverse_other(s, step)
                if s == STREAMS - 1:
                    load_inverse(step + 1)
                pair_sum(s)
                if not (exact and step == last_step):
                    cross(s)
            older(step + 1, [step - 1])
            load_factor(step + 1)

        outputs = []
        for step in range(steps_total):
            if exact and step == last_step:
                low = place < n_row // 2
                leaving = order.run(
                    lambda a, b: jnp.where(low, b, a), state[0]["leaving"], state[1]["leaving"]
                )
                arrived = trade(leaving, "row", 2)
                found = narrow(jnp.where(low, state[0]["total"], state[1]["total"]) + wide(arrived))
                outputs.append(found.T)
                continue
            if step == last_step:
                for s in range(STREAMS):
                    solve(s, step)
            unit = place * UNITS // n_row
            found = solved[step][0][0]
            for s in range(STREAMS):
                for u in range(2):
                    found = jnp.where(unit == 2 * s + (u ^ side), solved[step][s][u], found)
            if not exact:
                slot = angles // n_row
                found = lax.dynamic_slice_in_dim(found, (place * slot) % width, slot, 0)
            outputs.append(found.T)
        return jnp.stack(outputs, axis=0)

    return per_device


def solution(mesh):
    placed = (P("groups", "row", "col"), P("groups", "col", "row"), P("groups", "row", None))
    return jax.shard_map(
        make_per_device(mesh.shape["row"], mesh.shape["col"]),
        mesh=mesh,
        in_specs=placed,
        out_specs=P("groups", "col", "row"),
        check_vma=False,
    )
```

```python
import functools

import jax
import jax.numpy as jnp
from jax import lax
from jax.experimental import pallas as pl
from jax.experimental.pallas import tpu as pltpu
from jax.sharding import PartitionSpec as P

STREAMS = 2
UNITS = 2 * STREAMS


def pair_index(block_row, column_index):
    return block_row * (block_row - 1) // 2 + column_index


HBM = pl.BlockSpec(memory_space=pl.ANY)
VMEM = pl.BlockSpec(memory_space=pltpu.VMEM)
SMEM = pl.BlockSpec(memory_space=pltpu.SMEM)
COST = pl.CostEstimate(flops=1, bytes_accessed=1, transcendentals=0)


def params():
    return pltpu.CompilerParams(vmem_limit_bytes=16 * 2**20)


def times_transposed(left, right):
    return lax.dot_general(left, right, (((1,), (1,)), ((), ())), preferred_element_type=jnp.float32)


TILE = 256


def product_kernel(count, block, *refs):
    units, rest, out = refs[:count], refs[count:-1], refs[-1]
    x = units[0][...] if count == 1 else jnp.concatenate([u[...] for u in units], axis=0)
    rows = block.shape[0]
    tile = min(rows, TILE)
    for t in range(rows // tile):
        cut = pl.ds(t * tile, tile)
        value = times_transposed(block[cut], x).T
        for r in rest:
            value = value + r[:, cut]
        out[:, cut] = value.astype(out.dtype)


def product(block, units, rest=(), kind=jnp.float32):
    angles = sum(u.shape[0] for u in units)
    return pl.pallas_call(
        functools.partial(product_kernel, len(units)),
        out_shape=jax.ShapeDtypeStruct((angles, block.shape[0]), kind),
        in_specs=[VMEM] * (1 + len(units) + len(rest)),
        out_specs=VMEM,
        compiler_params=params(),
        cost_estimate=COST,
    )(block, *units, *rest)


def first_kernel(s, side, sides, blocks, keep, leave, product, right, held, sems, right_sem):
    width, rows = keep.shape
    tile = min(rows, TILE)
    bring = pltpu.make_async_copy(sides.at[0, :, pl.ds(2 * s * width, 2 * width)], right, right_sem)
    bring.start()
    copies = []
    for t in range(rows // tile):
        cut = pl.ds(t * tile, tile)
        copy = pltpu.make_async_copy(blocks.at[0, cut], held.at[cut], sems.at[t])
        copy.start()
        copies.append((cut, copy))
    bring.wait()
    x = right[...].T
    for cut, copy in copies:
        copy.wait()
        product[:, cut] = times_transposed(held[cut], x).T
    own = pl.multiple_of(side[0] * width, width)
    other = pl.multiple_of((1 - side[0]) * width, width)
    leave[...] = product[pl.ds(own, width)].astype(jnp.bfloat16)
    keep[...] = product[pl.ds(other, width)]


def first_products(s, side, sides, blocks):
    rows, depth = blocks.shape[1:]
    width = sides.shape[2] // UNITS
    return pl.pallas_call(
        functools.partial(first_kernel, s),
        out_shape=(
            jax.ShapeDtypeStruct((width, rows), jnp.float32),
            jax.ShapeDtypeStruct((width, rows), jnp.bfloat16),
        ),
        in_specs=[SMEM, HBM, HBM],
        out_specs=(VMEM, VMEM),
        scratch_shapes=[
            pltpu.VMEM((2 * width, rows), jnp.float32),
            pltpu.VMEM((depth, 2 * width), jnp.bfloat16),
            pltpu.VMEM((rows, depth), jnp.bfloat16),
            pltpu.SemaphoreType.DMA((rows // min(rows, TILE),)),
            pltpu.SemaphoreType.DMA,
        ],
        compiler_params=pltpu.CompilerParams(vmem_limit_bytes=56 * 2**20),
        cost_estimate=COST,
    )(side, sides, blocks)


def turn_kernel(width, side, sides, out, turned):
    turned[...] = sides[0].T
    for s in range(STREAMS):
        own = pl.multiple_of((2 * s + side[0]) * width, width)
        out[0, s] = turned[pl.ds(own, width)]


def turned_sides(side, sides):
    steps, rows, angles = sides.shape
    width = angles // UNITS
    return pl.pallas_call(
        functools.partial(turn_kernel, width),
        grid=(steps - 1,),
        out_shape=jax.ShapeDtypeStruct((steps - 1, STREAMS, width, rows), jnp.bfloat16),
        in_specs=[SMEM, pl.BlockSpec((1, rows, angles), lambda i: (i + 1, 0, 0))],
        out_specs=pl.BlockSpec((1, STREAMS, width, rows), lambda i: (i, 0, 0, 0)),
        scratch_shapes=[pltpu.VMEM((angles, rows), jnp.bfloat16)],
        compiler_params=params(),
        cost_estimate=COST,
    )(side, sides)


def wide(value):
    return value.astype(jnp.float32)


def narrow(value):
    return value.astype(jnp.bfloat16)


class Order:
    def __init__(self):
        self.last = None

    def run(self, work, *values):
        if self.last is not None:
            *values, _ = lax.optimization_barrier((*values, self.last))
        result = work(*values)
        self.last = result[0] if isinstance(result, (tuple, list)) else result
        return result

    def block(self, blocks, index):
        self.last = lax.optimization_barrier(self.run(lambda v: v[index], blocks))
        return self.last


def make_per_device(n_row, n_col):
    def trade(value, axis, step):
        size = n_row if axis == "row" else n_col
        return lax.ppermute(value, axis, [(i, i ^ step) for i in range(size)])

    def more_rounds(value, axis):
        size = n_row if axis == "row" else n_col
        step = 4
        while step < size:
            value = value + wide(trade(narrow(value), axis, step))
            step *= 2
        return value

    def per_device(factor_blocks, inverse_blocks, right_sides):
        steps_total, group_rows, angles = right_sides.shape
        last_step = steps_total - 1
        place = lax.axis_index("row")
        core = lax.axis_index("col") & 1
        side = (place & 1) ^ core
        side_ref = side.astype(jnp.int32).reshape(1)
        width = angles // UNITS
        exact = n_row == UNITS
        order = Order()
        solved = [[None] * STREAMS for _ in range(steps_total)]
        state = [dict() for _ in range(STREAMS)]
        sums = [None] * (steps_total + 1)
        factors = [None] * steps_total
        inverses = [None] * steps_total

        def load_factor(step):
            if step < steps_total:
                factors[step] = order.block(factor_blocks, pair_index(step, step - 1))

        def load_inverse(step):
            if step < steps_total:
                inverses[step] = order.block(inverse_blocks, step)

        def older(step, blocks):
            if step >= steps_total:
                return
            for j in blocks:
                block = order.block(factor_blocks, pair_index(step, j))
                units = [u for s in range(STREAMS) for u in solved[j][s]]

                rest = [] if sums[step] is None else [sums[step]]
                sums[step] = order.run(
                    lambda block, *v: product(block, v[: len(units)], v[len(units) :]), block, *units, *rest
                )

        def older_part(s, step, u):
            first = (2 * s + u) * width
            return [] if sums[step] is None else [sums[step][first : first + width]]

        def factor_other(s, step):
            st = state[s]
            leaving = order.run(
                lambda block, x, *rest: product(block, [x], rest, jnp.bfloat16),
                factors[step],
                solved[step - 1][s][1],
                *older_part(s, step, 1),
            )
            st["swap"] = trade(leaving, "col", 1)

        def factor_own(s, step):
            state[s]["sum"] = order.run(
                lambda block, x, *rest: product(block, [x], rest),
                factors[step],
                solved[step - 1][s][0],
                *older_part(s, step, 0),
            )

        def chip_sum(s):
            def work(value, arrived):
                value = value + wide(arrived)
                return narrow(value), value

            st = state[s]
            leaving, st["sum"] = order.run(work, st["sum"], st["swap"])
            st["flight"] = trade(leaving, "col", 2) if n_col > 2 else None

        def residual(s, step):
            def work(side_values, value, *arrived):
                for a in arrived:
                    value = more_rounds(value + wide(a), "col")
                return narrow(wide(side_values) - value)

            st = state[s]
            arrived = [] if st["flight"] is None else [st["flight"]]
            st["own"] = order.run(work, base[step - 1, s], st["sum"], *arrived)
            st["swap"] = trade(st["own"], "col", 1)

        def inverse_own(s, step):
            st = state[s]
            if exact and step == last_step:
                own, other = st["own"], st["swap"]
                st["own"], st["swap"] = jnp.where(core == 0, other, own), jnp.where(core == 0, own, other)
            leaving = order.run(
                lambda block, x: product(block, [x], kind=jnp.bfloat16), inverses[step], st["own"]
            )
            st["flight"] = trade(leaving, "row", 1)

        def inverse_other(s, step):
            st = state[s]
            st["total"] = order.run(lambda block, x: product(block, [x]), inverses[step], st["swap"])

        def pair_sum(s):
            def work(value, arrived):
                value = value + wide(arrived)
                return narrow(value), value

            st = state[s]
            st["leaving"], st["total"] = order.run(work, st["total"], st["flight"])

        def cross(s):
            st = state[s]
            st["flight"] = trade(st["leaving"], "row", 2) if n_row > 2 else None

        def solve(s, step):
            def work(value, *arrived):
                for a in arrived:
                    value = more_rounds(value + wide(a), "row")
                return narrow(value)

            st = state[s]
            arrived = [] if st["flight"] is None else [st["flight"]]
            other = order.run(work, st["total"], *arrived)
            solved[step][s] = (trade(other, "row", 1), other)

        for s in range(STREAMS):
            state[s]["total"], leaving = order.run(
                lambda v, w: first_products(s, side_ref, v, w), right_sides, inverse_blocks
            )
            state[s]["flight"] = trade(leaving, "row", 1)
        if steps_total > 1:
            base = order.run(lambda v: turned_sides(side_ref, v), right_sides)
        pair_sum(0)
        cross(0)
        load_factor(1)
        load_inverse(1)

        for step in range(1, steps_total):
            final = exact and step == last_step
            solve(0, step - 1)
            factor_other(0, step)
            pair_sum(1)
            cross(1)
            factor_own(0, step)
            chip_sum(0)
            older(step + 1, range(step - 1))
            if step == 1:
                load_factor(2)
            residual(0, step)
            inverse_own(0, step)
            solve(1, step - 1)
            factor_other(1, step)
            inverse_other(0, step)
            pair_sum(0)
            if not final:
                cross(0)
            factor_own(1, step)
            chip_sum(1)
            older(step + 1, [step - 1])
            if step > 1:
                load_factor(step + 1)
            residual(1, step)
            inverse_own(1, step)
            inverse_other(1, step)
            load_inverse(step + 1)
        pair_sum(1)

        outputs = []
        for step in range(steps_total):
            if exact and step == last_step:
                low = place < n_row // 2
                leaving = order.run(
                    lambda a, b: jnp.where(low, b, a), state[0]["leaving"], state[1]["leaving"]
                )
                arrived = trade(leaving, "row", 2)
                found = narrow(jnp.where(low, state[0]["total"], state[1]["total"]) + wide(arrived))
                outputs.append(found.T)
                continue
            if step == last_step:
                solve(0, step)
                cross(1)
                solve(1, step)
            unit = place * UNITS // n_row
            found = solved[step][0][0]
            for s in range(STREAMS):
                for u in range(2):
                    found = jnp.where(unit == 2 * s + (u ^ side), solved[step][s][u], found)
            if not exact:
                slot = angles // n_row
                found = lax.dynamic_slice_in_dim(found, (place * slot) % width, slot, 0)
            outputs.append(found.T)
        return jnp.stack(outputs, axis=0)

    return per_device


def solution(mesh):
    placed = (P("groups", "row", "col"), P("groups", "col", "row"), P("groups", "row", None))
    return jax.shard_map(
        make_per_device(mesh.shape["row"], mesh.shape["col"]),
        mesh=mesh,
        in_specs=placed,
        out_specs=P("groups", "col", "row"),
        check_vma=False,
    )
```

```python
import functools

import jax
import jax.numpy as jnp
from jax import lax
from jax.experimental import pallas as pl
from jax.experimental.pallas import tpu as pltpu
from jax.sharding import PartitionSpec as P

STREAMS = 2
UNITS = 2 * STREAMS


def pair_index(block_row, column_index):
    return block_row * (block_row - 1) // 2 + column_index


VMEM = pl.BlockSpec(memory_space=pltpu.VMEM)
SMEM = pl.BlockSpec(memory_space=pltpu.SMEM)
COST = pl.CostEstimate(flops=1, bytes_accessed=1, transcendentals=0)


def params():
    return pltpu.CompilerParams(vmem_limit_bytes=8 * 2**20)


def times_transposed(left, right):
    return lax.dot_general(left, right, (((1,), (1,)), ((), ())), preferred_element_type=jnp.float32)


TILE = 256


def product_kernel(count, block, *refs):
    units, rest, out = refs[:count], refs[count:-1], refs[-1]
    x = units[0][...] if count == 1 else jnp.concatenate([u[...] for u in units], axis=0)
    rows = block.shape[0]
    tile = min(rows, TILE)
    for t in range(rows // tile):
        cut = pl.ds(t * tile, tile)
        value = times_transposed(block[cut], x).T
        for r in rest:
            value = value + r[:, cut]
        out[:, cut] = value.astype(out.dtype)


def product(block, units, rest=(), kind=jnp.float32):
    angles = sum(u.shape[0] for u in units)
    return pl.pallas_call(
        functools.partial(product_kernel, len(units)),
        out_shape=jax.ShapeDtypeStruct((angles, block.shape[0]), kind),
        in_specs=[VMEM] * (1 + len(units) + len(rest)),
        out_specs=VMEM,
        compiler_params=params(),
        cost_estimate=COST,
    )(block, *units, *rest)


def first_kernel(s, side, right, block, keep, leave, product):
    width = keep.shape[0]
    x = right[:, pl.ds(2 * s * width, 2 * width)].T
    product[...] = times_transposed(x, block[...])
    own = pl.multiple_of(side[0] * width, width)
    other = pl.multiple_of((1 - side[0]) * width, width)
    leave[...] = product[pl.ds(own, width)].astype(jnp.bfloat16)
    keep[...] = product[pl.ds(other, width)]


def first_products(s, side, right, block):
    rows = block.shape[0]
    width = right.shape[1] // UNITS
    return pl.pallas_call(
        functools.partial(first_kernel, s),
        out_shape=(
            jax.ShapeDtypeStruct((width, rows), jnp.float32),
            jax.ShapeDtypeStruct((width, rows), jnp.bfloat16),
        ),
        in_specs=[SMEM, VMEM, VMEM],
        out_specs=(VMEM, VMEM),
        scratch_shapes=[pltpu.VMEM((2 * width, rows), jnp.float32)],
        compiler_params=params(),
        cost_estimate=COST,
    )(side, right, block)


def turn_kernel(width, side, sides, out, turned):
    turned[...] = sides[0].T
    for s in range(STREAMS):
        own = pl.multiple_of((2 * s + side[0]) * width, width)
        out[0, s] = turned[pl.ds(own, width)]


def turned_sides(side, sides):
    steps, rows, angles = sides.shape
    width = angles // UNITS
    return pl.pallas_call(
        functools.partial(turn_kernel, width),
        grid=(steps - 1,),
        out_shape=jax.ShapeDtypeStruct((steps - 1, STREAMS, width, rows), jnp.bfloat16),
        in_specs=[SMEM, pl.BlockSpec((1, rows, angles), lambda i: (i + 1, 0, 0))],
        out_specs=pl.BlockSpec((1, STREAMS, width, rows), lambda i: (i, 0, 0, 0)),
        scratch_shapes=[pltpu.VMEM((angles, rows), jnp.bfloat16)],
        compiler_params=params(),
        cost_estimate=COST,
    )(side, sides)


def wide(value):
    return value.astype(jnp.float32)


def narrow(value):
    return value.astype(jnp.bfloat16)


class Order:
    def __init__(self):
        self.last = None

    def run(self, work, *values):
        if self.last is not None:
            *values, _ = lax.optimization_barrier((*values, self.last))
        result = work(*values)
        self.last = result[0] if isinstance(result, (tuple, list)) else result
        return result

    def block(self, blocks, index):
        self.last = lax.optimization_barrier(self.run(lambda v: v[index], blocks))
        return self.last


def make_per_device(n_row, n_col):
    def trade(value, axis, step):
        size = n_row if axis == "row" else n_col
        return lax.ppermute(value, axis, [(i, i ^ step) for i in range(size)])

    def more_rounds(value, axis):
        size = n_row if axis == "row" else n_col
        step = 4
        while step < size:
            value = value + wide(trade(narrow(value), axis, step))
            step *= 2
        return value

    def per_device(factor_blocks, inverse_blocks, right_sides):
        steps_total, group_rows, angles = right_sides.shape
        last_step = steps_total - 1
        place = lax.axis_index("row")
        core = lax.axis_index("col") & 1
        side = (place & 1) ^ core
        side_ref = side.astype(jnp.int32).reshape(1)
        width = angles // UNITS
        exact = n_row == UNITS
        order = Order()
        solved = [[None] * STREAMS for _ in range(steps_total)]
        state = [dict() for _ in range(STREAMS)]
        sums = [None] * (steps_total + 1)
        factors = [None] * steps_total
        inverses = [None] * steps_total

        def load_factor(step):
            if step < steps_total:
                factors[step] = order.block(factor_blocks, pair_index(step, step - 1))

        def load_inverse(step):
            if step < steps_total:
                inverses[step] = order.block(inverse_blocks, step)

        def older(step, blocks):
            if step >= steps_total:
                return
            for j in blocks:
                block = order.block(factor_blocks, pair_index(step, j))
                units = [u for s in range(STREAMS) for u in solved[j][s]]

                rest = [] if sums[step] is None else [sums[step]]
                sums[step] = order.run(
                    lambda block, *v: product(block, v[: len(units)], v[len(units) :]), block, *units, *rest
                )

        def older_part(s, step, u):
            first = (2 * s + u) * width
            return [] if sums[step] is None else [sums[step][first : first + width]]

        def factor_other(s, step):
            st = state[s]
            leaving = order.run(
                lambda block, x, *rest: product(block, [x], rest, jnp.bfloat16),
                factors[step],
                solved[step - 1][s][1],
                *older_part(s, step, 1),
            )
            st["swap"] = trade(leaving, "col", 1)

        def factor_own(s, step):
            state[s]["sum"] = order.run(
                lambda block, x, *rest: product(block, [x], rest),
                factors[step],
                solved[step - 1][s][0],
                *older_part(s, step, 0),
            )

        def chip_sum(s):
            def work(value, arrived):
                value = value + wide(arrived)
                return narrow(value), value

            st = state[s]
            leaving, st["sum"] = order.run(work, st["sum"], st["swap"])
            st["flight"] = trade(leaving, "col", 2) if n_col > 2 else None

        def residual(s, step):
            def work(side_values, value, *arrived):
                for a in arrived:
                    value = more_rounds(value + wide(a), "col")
                return narrow(wide(side_values) - value)

            st = state[s]
            arrived = [] if st["flight"] is None else [st["flight"]]
            st["own"] = order.run(work, base[step - 1, s], st["sum"], *arrived)
            st["swap"] = trade(st["own"], "col", 1)

        def inverse_own(s, step):
            st = state[s]
            if exact and step == last_step:
                own, other = st["own"], st["swap"]
                st["own"], st["swap"] = jnp.where(core == 0, other, own), jnp.where(core == 0, own, other)
            leaving = order.run(
                lambda block, x: product(block, [x], kind=jnp.bfloat16), inverses[step], st["own"]
            )
            st["flight"] = trade(leaving, "row", 1)

        def inverse_other(s, step):
            st = state[s]
            st["total"] = order.run(lambda block, x: product(block, [x]), inverses[step], st["swap"])

        def pair_sum(s):
            def work(value, arrived):
                value = value + wide(arrived)
                return narrow(value), value

            st = state[s]
            st["leaving"], st["total"] = order.run(work, st["total"], st["flight"])

        def cross(s):
            st = state[s]
            st["flight"] = trade(st["leaving"], "row", 2) if n_row > 2 else None

        def solve(s, step):
            def work(value, *arrived):
                for a in arrived:
                    value = more_rounds(value + wide(a), "row")
                return narrow(value)

            st = state[s]
            arrived = [] if st["flight"] is None else [st["flight"]]
            other = order.run(work, st["total"], *arrived)
            solved[step][s] = (trade(other, "row", 1), other)

        inverses[0] = order.block(inverse_blocks, 0)
        right = order.block(right_sides, 0)
        for s in range(STREAMS):
            state[s]["total"], leaving = order.run(
                lambda v, w: first_products(s, side_ref, v, w), right, inverses[0]
            )
            state[s]["flight"] = trade(leaving, "row", 1)
        if steps_total > 1:
            base = order.run(lambda v: turned_sides(side_ref, v), right_sides)
        pair_sum(0)
        cross(0)
        load_factor(1)
        load_inverse(1)

        for step in range(1, steps_total):
            final = exact and step == last_step
            solve(0, step - 1)
            factor_other(0, step)
            pair_sum(1)
            cross(1)
            factor_own(0, step)
            chip_sum(0)
            solve(1, step - 1)
            factor_other(1, step)
            older(step + 1, range(step - 1))
            load_factor(step + 1)
            load_inverse(step + 1)
            residual(0, step)
            inverse_own(0, step)
            factor_own(1, step)
            chip_sum(1)
            older(step + 1, [step - 1])
            inverse_other(0, step)
            pair_sum(0)
            if not final:
                cross(0)
            residual(1, step)
            inverse_own(1, step)
            inverse_other(1, step)
        pair_sum(1)

        outputs = []
        for step in range(steps_total):
            if exact and step == last_step:
                low = place < n_row // 2
                leaving = order.run(
                    lambda a, b: jnp.where(low, b, a), state[0]["leaving"], state[1]["leaving"]
                )
                arrived = trade(leaving, "row", 2)
                found = narrow(jnp.where(low, state[0]["total"], state[1]["total"]) + wide(arrived))
                outputs.append(found.T)
                continue
            if step == last_step:
                solve(0, step)
                cross(1)
                solve(1, step)
            unit = place * UNITS // n_row
            found = solved[step][0][0]
            for s in range(STREAMS):
                for u in range(2):
                    found = jnp.where(unit == 2 * s + (u ^ side), solved[step][s][u], found)
            if not exact:
                slot = angles // n_row
                found = lax.dynamic_slice_in_dim(found, (place * slot) % width, slot, 0)
            outputs.append(found.T)
        return jnp.stack(outputs, axis=0)

    return per_device


def solution(mesh):
    placed = (P("groups", "row", "col"), P("groups", "col", "row"), P("groups", "row", None))
    return jax.shard_map(
        make_per_device(mesh.shape["row"], mesh.shape["col"]),
        mesh=mesh,
        in_specs=placed,
        out_specs=P("groups", "col", "row"),
        check_vma=False,
    )
```

```python
import functools

import jax
import jax.numpy as jnp
from jax import lax
from jax.experimental import pallas as pl
from jax.experimental.pallas import tpu as pltpu
from jax.sharding import PartitionSpec as P

STREAMS = 2
UNITS = 2 * STREAMS


def pair_index(block_row, column_index):
    return block_row * (block_row - 1) // 2 + column_index


VMEM = pl.BlockSpec(memory_space=pltpu.VMEM)
SMEM = pl.BlockSpec(memory_space=pltpu.SMEM)
COST = pl.CostEstimate(flops=1, bytes_accessed=1, transcendentals=0)


def params():
    return pltpu.CompilerParams(vmem_limit_bytes=8 * 2**20)


def times_transposed(left, right):
    return lax.dot_general(left, right, (((1,), (1,)), ((), ())), preferred_element_type=jnp.float32)


TILE = 256


def product_kernel(count, block, *refs):
    units, rest, out = refs[:count], refs[count:-1], refs[-1]
    x = units[0][...] if count == 1 else jnp.concatenate([u[...] for u in units], axis=0)
    rows = block.shape[0]
    tile = min(rows, TILE)
    for t in range(rows // tile):
        cut = pl.ds(t * tile, tile)
        value = times_transposed(block[cut], x).T
        for r in rest:
            value = value + r[:, cut]
        out[:, cut] = value.astype(out.dtype)


def product(block, units, rest=(), kind=jnp.float32):
    angles = sum(u.shape[0] for u in units)
    return pl.pallas_call(
        functools.partial(product_kernel, len(units)),
        out_shape=jax.ShapeDtypeStruct((angles, block.shape[0]), kind),
        in_specs=[VMEM] * (1 + len(units) + len(rest)),
        out_specs=VMEM,
        compiler_params=params(),
        cost_estimate=COST,
    )(block, *units, *rest)


def first_kernel(s, side, right, block, keep, leave, product):
    width = keep.shape[0]
    x = right[:, pl.ds(2 * s * width, 2 * width)].T
    product[...] = times_transposed(x, block[...])
    own = pl.multiple_of(side[0] * width, width)
    other = pl.multiple_of((1 - side[0]) * width, width)
    leave[...] = product[pl.ds(own, width)].astype(jnp.bfloat16)
    keep[...] = product[pl.ds(other, width)]


def first_products(s, side, right, block):
    rows = block.shape[0]
    width = right.shape[1] // UNITS
    return pl.pallas_call(
        functools.partial(first_kernel, s),
        out_shape=(
            jax.ShapeDtypeStruct((width, rows), jnp.float32),
            jax.ShapeDtypeStruct((width, rows), jnp.bfloat16),
        ),
        in_specs=[SMEM, VMEM, VMEM],
        out_specs=(VMEM, VMEM),
        scratch_shapes=[pltpu.VMEM((2 * width, rows), jnp.float32)],
        compiler_params=params(),
        cost_estimate=COST,
    )(side, right, block)


def turn_kernel(width, side, sides, out, turned):
    turned[...] = sides[0].T
    for s in range(STREAMS):
        own = pl.multiple_of((2 * s + side[0]) * width, width)
        out[0, s] = turned[pl.ds(own, width)]


def turned_sides(side, sides):
    steps, rows, angles = sides.shape
    width = angles // UNITS
    return pl.pallas_call(
        functools.partial(turn_kernel, width),
        grid=(steps - 1,),
        out_shape=jax.ShapeDtypeStruct((steps - 1, STREAMS, width, rows), jnp.bfloat16),
        in_specs=[SMEM, pl.BlockSpec((1, rows, angles), lambda i: (i + 1, 0, 0))],
        out_specs=pl.BlockSpec((1, STREAMS, width, rows), lambda i: (i, 0, 0, 0)),
        scratch_shapes=[pltpu.VMEM((angles, rows), jnp.bfloat16)],
        compiler_params=params(),
        cost_estimate=COST,
    )(side, sides)


def wide(value):
    return value.astype(jnp.float32)


def narrow(value):
    return value.astype(jnp.bfloat16)


class Order:
    def __init__(self):
        self.last = None

    def run(self, work, *values):
        if self.last is not None:
            *values, _ = lax.optimization_barrier((*values, self.last))
        result = work(*values)
        self.last = result[0] if isinstance(result, (tuple, list)) else result
        return result

    def block(self, blocks, index):
        self.last = lax.optimization_barrier(self.run(lambda v: v[index], blocks))
        return self.last


def make_per_device(n_row, n_col):
    def trade(value, axis, step):
        size = n_row if axis == "row" else n_col
        return lax.ppermute(value, axis, [(i, i ^ step) for i in range(size)])

    def more_rounds(value, axis):
        size = n_row if axis == "row" else n_col
        step = 4
        while step < size:
            value = value + wide(trade(narrow(value), axis, step))
            step *= 2
        return value

    def per_device(factor_blocks, inverse_blocks, right_sides):
        steps_total, group_rows, angles = right_sides.shape
        last_step = steps_total - 1
        place = lax.axis_index("row")
        core = lax.axis_index("col") & 1
        side = (place & 1) ^ core
        side_ref = side.astype(jnp.int32).reshape(1)
        width = angles // UNITS
        exact = n_row == UNITS
        order = Order()
        solved = [[None] * STREAMS for _ in range(steps_total)]
        state = [dict() for _ in range(STREAMS)]
        sums = [None] * (steps_total + 1)
        factors = [None] * steps_total
        inverses = [None] * steps_total

        def load_factor(step):
            if step < steps_total:
                factors[step] = order.block(factor_blocks, pair_index(step, step - 1))

        def load_inverse(step):
            if step < steps_total:
                inverses[step] = order.block(inverse_blocks, step)

        def older(step, blocks):
            if step >= steps_total:
                return
            for j in blocks:
                block = order.block(factor_blocks, pair_index(step, j))
                units = [u for s in range(STREAMS) for u in solved[j][s]]

                rest = [] if sums[step] is None else [sums[step]]
                sums[step] = order.run(
                    lambda block, *v: product(block, v[: len(units)], v[len(units) :]), block, *units, *rest
                )

        def older_part(s, step, u):
            first = (2 * s + u) * width
            return [] if sums[step] is None else [sums[step][first : first + width]]

        def factor_other(s, step):
            st = state[s]
            leaving = order.run(
                lambda block, x, *rest: product(block, [x], rest, jnp.bfloat16),
                factors[step],
                solved[step - 1][s][1],
                *older_part(s, step, 1),
            )
            st["swap"] = trade(leaving, "col", 1)

        def factor_own(s, step):
            state[s]["sum"] = order.run(
                lambda block, x, *rest: product(block, [x], rest),
                factors[step],
                solved[step - 1][s][0],
                *older_part(s, step, 0),
            )

        def chip_sum(s):
            def work(value, arrived):
                value = value + wide(arrived)
                return narrow(value), value

            st = state[s]
            leaving, st["sum"] = order.run(work, st["sum"], st["swap"])
            st["flight"] = trade(leaving, "col", 2) if n_col > 2 else None

        def residual(s, step):
            def work(side_values, value, *arrived):
                for a in arrived:
                    value = more_rounds(value + wide(a), "col")
                return narrow(wide(side_values) - value)

            st = state[s]
            arrived = [] if st["flight"] is None else [st["flight"]]
            st["own"] = order.run(work, base[step - 1, s], st["sum"], *arrived)
            st["swap"] = trade(st["own"], "col", 1)

        def inverse_own(s, step):
            st = state[s]
            if exact and step == last_step:
                own, other = st["own"], st["swap"]
                st["own"], st["swap"] = jnp.where(core == 0, other, own), jnp.where(core == 0, own, other)
            leaving = order.run(
                lambda block, x: product(block, [x], kind=jnp.bfloat16), inverses[step], st["own"]
            )
            st["flight"] = trade(leaving, "row", 1)

        def inverse_other(s, step):
            st = state[s]
            st["total"] = order.run(lambda block, x: product(block, [x]), inverses[step], st["swap"])

        def pair_sum(s):
            def work(value, arrived):
                value = value + wide(arrived)
                return narrow(value), value

            st = state[s]
            st["leaving"], st["total"] = order.run(work, st["total"], st["flight"])

        def cross(s):
            st = state[s]
            st["flight"] = trade(st["leaving"], "row", 2) if n_row > 2 else None

        def solve(s, step):
            def work(value, *arrived):
                for a in arrived:
                    value = more_rounds(value + wide(a), "row")
                return narrow(value)

            st = state[s]
            arrived = [] if st["flight"] is None else [st["flight"]]
            other = order.run(work, st["total"], *arrived)
            solved[step][s] = (trade(other, "row", 1), other)

        inverses[0] = order.block(inverse_blocks, 0)
        right = order.block(right_sides, 0)
        def first(s):
            state[s]["total"], leaving = order.run(
                lambda v, w: first_products(s, side_ref, v, w), right, inverses[0]
            )
            state[s]["flight"] = trade(leaving, "row", 1)

        first(0)
        if steps_total > 1:
            base = order.run(lambda v: turned_sides(side_ref, v), right_sides)
            load_factor(1)
        pair_sum(0)
        cross(0)
        first(1)
        load_inverse(1)

        for step in range(1, steps_total):
            final = exact and step == last_step
            solve(0, step - 1)
            factor_other(0, step)
            pair_sum(1)
            cross(1)
            factor_own(0, step)
            chip_sum(0)
            older(step + 1, range(step - 1))
            load_factor(step + 1)
            load_inverse(step + 1)
            solve(1, step - 1)
            factor_other(1, step)
            residual(0, step)
            inverse_own(0, step)
            factor_own(1, step)
            chip_sum(1)
            older(step + 1, [step - 1])
            inverse_other(0, step)
            pair_sum(0)
            if not final:
                cross(0)
            residual(1, step)
            inverse_own(1, step)
            inverse_other(1, step)
        pair_sum(1)

        outputs = []
        for step in range(steps_total):
            if exact and step == last_step:
                low = place < n_row // 2
                leaving = order.run(
                    lambda a, b: jnp.where(low, b, a), state[0]["leaving"], state[1]["leaving"]
                )
                arrived = trade(leaving, "row", 2)
                found = narrow(jnp.where(low, state[0]["total"], state[1]["total"]) + wide(arrived))
                outputs.append(found.T)
                continue
            if step == last_step:
                solve(0, step)
                cross(1)
                solve(1, step)
            unit = place * UNITS // n_row
            found = solved[step][0][0]
            for s in range(STREAMS):
                for u in range(2):
                    found = jnp.where(unit == 2 * s + (u ^ side), solved[step][s][u], found)
            if not exact:
                slot = angles // n_row
                found = lax.dynamic_slice_in_dim(found, (place * slot) % width, slot, 0)
            outputs.append(found.T)
        return jnp.stack(outputs, axis=0)

    return per_device


def solution(mesh):
    placed = (P("groups", "row", "col"), P("groups", "col", "row"), P("groups", "row", None))
    return jax.shard_map(
        make_per_device(mesh.shape["row"], mesh.shape["col"]),
        mesh=mesh,
        in_specs=placed,
        out_specs=P("groups", "col", "row"),
        check_vma=False,
    )
```

```python
import functools

import jax
import jax.numpy as jnp
from jax import lax
from jax.experimental import pallas as pl
from jax.experimental.pallas import tpu as pltpu
from jax.sharding import PartitionSpec as P

STREAMS = 2
UNITS = 2 * STREAMS


def pair_index(block_row, column_index):
    return block_row * (block_row - 1) // 2 + column_index


VMEM = pl.BlockSpec(memory_space=pltpu.VMEM)
SMEM = pl.BlockSpec(memory_space=pltpu.SMEM)
COST = pl.CostEstimate(flops=1, bytes_accessed=1, transcendentals=0)


def params():
    return pltpu.CompilerParams(vmem_limit_bytes=8 * 2**20)


def times_transposed(left, right):
    return lax.dot_general(left, right, (((1,), (1,)), ((), ())), preferred_element_type=jnp.float32)


TILE = 256


def product_kernel(count, block, *refs):
    units, rest, out = refs[:count], refs[count:-1], refs[-1]
    x = units[0][...] if count == 1 else jnp.concatenate([u[...] for u in units], axis=0)
    rows = block.shape[0]
    tile = min(rows, TILE)
    for t in range(rows // tile):
        cut = pl.ds(t * tile, tile)
        value = times_transposed(block[cut], x).T
        for r in rest:
            value = value + r[:, cut]
        out[:, cut] = value.astype(out.dtype)


def product(block, units, rest=(), kind=jnp.float32):
    angles = sum(u.shape[0] for u in units)
    return pl.pallas_call(
        functools.partial(product_kernel, len(units)),
        out_shape=jax.ShapeDtypeStruct((angles, block.shape[0]), kind),
        in_specs=[VMEM] * (1 + len(units) + len(rest)),
        out_specs=VMEM,
        compiler_params=params(),
        cost_estimate=COST,
    )(block, *units, *rest)


def first_kernel(s, side, right, block, keep, leave, product):
    width = keep.shape[0]
    x = right[:, pl.ds(2 * s * width, 2 * width)].T
    product[...] = times_transposed(x, block[...])
    own = pl.multiple_of(side[0] * width, width)
    other = pl.multiple_of((1 - side[0]) * width, width)
    leave[...] = product[pl.ds(own, width)].astype(jnp.bfloat16)
    keep[...] = product[pl.ds(other, width)]


def first_products(s, side, right, block):
    rows = block.shape[0]
    width = right.shape[1] // UNITS
    return pl.pallas_call(
        functools.partial(first_kernel, s),
        out_shape=(
            jax.ShapeDtypeStruct((width, rows), jnp.float32),
            jax.ShapeDtypeStruct((width, rows), jnp.bfloat16),
        ),
        in_specs=[SMEM, VMEM, VMEM],
        out_specs=(VMEM, VMEM),
        scratch_shapes=[pltpu.VMEM((2 * width, rows), jnp.float32)],
        compiler_params=params(),
        cost_estimate=COST,
    )(side, right, block)


def turn_kernel(width, side, sides, out, turned):
    turned[...] = sides[0].T
    for s in range(STREAMS):
        own = pl.multiple_of((2 * s + side[0]) * width, width)
        out[0, s] = turned[pl.ds(own, width)]


def turned_sides(side, sides):
    steps, rows, angles = sides.shape
    width = angles // UNITS
    return pl.pallas_call(
        functools.partial(turn_kernel, width),
        grid=(steps - 1,),
        out_shape=jax.ShapeDtypeStruct((steps - 1, STREAMS, width, rows), jnp.bfloat16),
        in_specs=[SMEM, pl.BlockSpec((1, rows, angles), lambda i: (i + 1, 0, 0))],
        out_specs=pl.BlockSpec((1, STREAMS, width, rows), lambda i: (i, 0, 0, 0)),
        scratch_shapes=[pltpu.VMEM((angles, rows), jnp.bfloat16)],
        compiler_params=params(),
        cost_estimate=COST,
    )(side, sides)


def wide(value):
    return value.astype(jnp.float32)


def narrow(value):
    return value.astype(jnp.bfloat16)


class Order:
    def __init__(self):
        self.last = None

    def run(self, work, *values):
        if self.last is not None:
            *values, _ = lax.optimization_barrier((*values, self.last))
        result = work(*values)
        self.last = result[0] if isinstance(result, (tuple, list)) else result
        return result

    def block(self, blocks, index):
        self.last = lax.optimization_barrier(self.run(lambda v: v[index], blocks))
        return self.last


def make_per_device(n_row, n_col):
    def trade(value, axis, step):
        size = n_row if axis == "row" else n_col
        return lax.ppermute(value, axis, [(i, i ^ step) for i in range(size)])

    def more_rounds(value, axis):
        size = n_row if axis == "row" else n_col
        step = 4
        while step < size:
            value = value + wide(trade(narrow(value), axis, step))
            step *= 2
        return value

    def per_device(factor_blocks, inverse_blocks, right_sides):
        steps_total, group_rows, angles = right_sides.shape
        last_step = steps_total - 1
        place = lax.axis_index("row")
        core = lax.axis_index("col") & 1
        side = (place & 1) ^ core
        side_ref = side.astype(jnp.int32).reshape(1)
        width = angles // UNITS
        exact = n_row == UNITS
        order = Order()
        solved = [[None] * STREAMS for _ in range(steps_total)]
        state = [dict() for _ in range(STREAMS)]
        sums = [[None] * STREAMS for _ in range(steps_total)]
        factors = [None] * steps_total
        inverses = [None] * steps_total

        def load_factor(step):
            if step < steps_total:
                factors[step] = order.block(factor_blocks, pair_index(step, step - 1))

        def load_inverse(step):
            if step < steps_total:
                inverses[step] = order.block(inverse_blocks, step)

        def older(s, step, blocks):
            if step >= steps_total:
                return
            for j in blocks:
                block = order.block(factor_blocks, pair_index(step, j))
                rest = [] if sums[step][s] is None else [sums[step][s]]
                sums[step][s] = order.run(
                    lambda block, own, other, *rest: product(block, [own, other], rest),
                    block,
                    *solved[j][s],
                    *rest,
                )

        def older_part(s, step, u):
            return [] if sums[step][s] is None else [sums[step][s][u * width : (u + 1) * width]]

        def factor_other(s, step):
            st = state[s]
            leaving = order.run(
                lambda block, x, *rest: product(block, [x], rest, jnp.bfloat16),
                factors[step],
                solved[step - 1][s][1],
                *older_part(s, step, 1),
            )
            st["swap"] = trade(leaving, "col", 1)

        def factor_own(s, step):
            state[s]["sum"] = order.run(
                lambda block, x, *rest: product(block, [x], rest),
                factors[step],
                solved[step - 1][s][0],
                *older_part(s, step, 0),
            )

        def chip_sum(s):
            def work(value, arrived):
                value = value + wide(arrived)
                return narrow(value), value

            st = state[s]
            leaving, st["sum"] = order.run(work, st["sum"], st["swap"])
            st["flight"] = trade(leaving, "col", 2) if n_col > 2 else None

        def residual(s, step):
            def work(side_values, value, *arrived):
                for a in arrived:
                    value = more_rounds(value + wide(a), "col")
                return narrow(wide(side_values) - value)

            st = state[s]
            arrived = [] if st["flight"] is None else [st["flight"]]
            st["own"] = order.run(work, base[step - 1, s], st["sum"], *arrived)
            st["swap"] = trade(st["own"], "col", 1)

        def inverse_own(s, step):
            st = state[s]
            if exact and step == last_step:
                own, other = st["own"], st["swap"]
                st["own"], st["swap"] = jnp.where(core == 0, other, own), jnp.where(core == 0, own, other)
            leaving = order.run(
                lambda block, x: product(block, [x], kind=jnp.bfloat16), inverses[step], st["own"]
            )
            st["flight"] = trade(leaving, "row", 1)

        def inverse_other(s, step):
            st = state[s]
            st["total"] = order.run(lambda block, x: product(block, [x]), inverses[step], st["swap"])

        def pair_sum(s):
            def work(value, arrived):
                value = value + wide(arrived)
                return narrow(value), value

            st = state[s]
            st["leaving"], st["total"] = order.run(work, st["total"], st["flight"])

        def cross(s):
            st = state[s]
            st["flight"] = trade(st["leaving"], "row", 2) if n_row > 2 else None

        def solve(s, step):
            def work(value, *arrived):
                for a in arrived:
                    value = more_rounds(value + wide(a), "row")
                return narrow(value)

            st = state[s]
            arrived = [] if st["flight"] is None else [st["flight"]]
            other = order.run(work, st["total"], *arrived)
            solved[step][s] = (trade(other, "row", 1), other)

        inverses[0] = order.block(inverse_blocks, 0)
        right = order.block(right_sides, 0)
        def first(s):
            state[s]["total"], leaving = order.run(
                lambda v, w: first_products(s, side_ref, v, w), right, inverses[0]
            )
            state[s]["flight"] = trade(leaving, "row", 1)

        first(0)
        if steps_total > 1:
            base = order.run(lambda v: turned_sides(side_ref, v), right_sides)
        pair_sum(0)
        cross(0)
        first(1)
        load_factor(1)
        load_inverse(1)

        for step in range(1, steps_total):
            final = exact and step == last_step
            solve(0, step - 1)
            factor_other(0, step)
            load_inverse(step + 1)
            pair_sum(1)
            cross(1)
            older(1, step, range(step - 1))
            factor_own(0, step)
            chip_sum(0)
            older(0, step + 1, range(step))
            load_factor(step + 1)
            if step == last_step:
                residual(0, step)
            solve(1, step - 1)
            factor_other(1, step)
            if step < last_step:
                residual(0, step)
            inverse_own(0, step)
            factor_own(1, step)
            chip_sum(1)
            inverse_other(0, step)
            pair_sum(0)
            if not final:
                cross(0)
            residual(1, step)
            inverse_own(1, step)
            inverse_other(1, step)
        pair_sum(1)

        outputs = []
        for step in range(steps_total):
            if exact and step == last_step:
                low = place < n_row // 2
                leaving = order.run(
                    lambda a, b: jnp.where(low, b, a), state[0]["leaving"], state[1]["leaving"]
                )
                arrived = trade(leaving, "row", 2)
                found = narrow(jnp.where(low, state[0]["total"], state[1]["total"]) + wide(arrived))
                outputs.append(found.T)
                continue
            if step == last_step:
                solve(0, step)
                cross(1)
                solve(1, step)
            unit = place * UNITS // n_row
            found = solved[step][0][0]
            for s in range(STREAMS):
                for u in range(2):
                    found = jnp.where(unit == 2 * s + (u ^ side), solved[step][s][u], found)
            if not exact:
                slot = angles // n_row
                found = lax.dynamic_slice_in_dim(found, (place * slot) % width, slot, 0)
            outputs.append(found.T)
        return jnp.stack(outputs, axis=0)

    return per_device


def solution(mesh):
    placed = (P("groups", "row", "col"), P("groups", "col", "row"), P("groups", "row", None))
    return jax.shard_map(
        make_per_device(mesh.shape["row"], mesh.shape["col"]),
        mesh=mesh,
        in_specs=placed,
        out_specs=P("groups", "col", "row"),
        check_vma=False,
    )
```

```python
import functools

import jax
import jax.numpy as jnp
from jax import lax
from jax.experimental import pallas as pl
from jax.experimental.pallas import tpu as pltpu
from jax.sharding import PartitionSpec as P

STREAMS = 2
UNITS = 2 * STREAMS


def pair_index(block_row, column_index):
    return block_row * (block_row - 1) // 2 + column_index


VMEM = pl.BlockSpec(memory_space=pltpu.VMEM)
SMEM = pl.BlockSpec(memory_space=pltpu.SMEM)
COST = pl.CostEstimate(flops=1, bytes_accessed=1, transcendentals=0)


def params():
    return pltpu.CompilerParams(vmem_limit_bytes=8 * 2**20)


def times_transposed(left, right):
    return lax.dot_general(left, right, (((1,), (1,)), ((), ())), preferred_element_type=jnp.float32)


TILE = 256


def product_kernel(count, block, *refs):
    units, rest, out = refs[:count], refs[count:-1], refs[-1]
    x = units[0][...] if count == 1 else jnp.concatenate([u[...] for u in units], axis=0)
    rows = block.shape[0]
    tile = min(rows, TILE)
    for t in range(rows // tile):
        cut = pl.ds(t * tile, tile)
        value = times_transposed(block[cut], x).T
        for r in rest:
            value = value + r[:, cut]
        out[:, cut] = value.astype(out.dtype)


def product(block, units, rest=(), kind=jnp.float32):
    angles = sum(u.shape[0] for u in units)
    return pl.pallas_call(
        functools.partial(product_kernel, len(units)),
        out_shape=jax.ShapeDtypeStruct((angles, block.shape[0]), kind),
        in_specs=[VMEM] * (1 + len(units) + len(rest)),
        out_specs=VMEM,
        compiler_params=params(),
        cost_estimate=COST,
    )(block, *units, *rest)


def first_kernel(s, side, right, block, keep, leave, product):
    width = keep.shape[0]
    x = right[:, pl.ds(2 * s * width, 2 * width)].T
    product[...] = times_transposed(x, block[...])
    own = pl.multiple_of(side[0] * width, width)
    other = pl.multiple_of((1 - side[0]) * width, width)
    leave[...] = product[pl.ds(own, width)].astype(jnp.bfloat16)
    keep[...] = product[pl.ds(other, width)]


def first_products(s, side, right, block):
    rows = block.shape[0]
    width = right.shape[1] // UNITS
    return pl.pallas_call(
        functools.partial(first_kernel, s),
        out_shape=(
            jax.ShapeDtypeStruct((width, rows), jnp.float32),
            jax.ShapeDtypeStruct((width, rows), jnp.bfloat16),
        ),
        in_specs=[SMEM, VMEM, VMEM],
        out_specs=(VMEM, VMEM),
        scratch_shapes=[pltpu.VMEM((2 * width, rows), jnp.float32)],
        compiler_params=params(),
        cost_estimate=COST,
    )(side, right, block)


def turn_kernel(side, sides, *refs):
    outs, turned = refs[:STREAMS], refs[STREAMS]
    width = outs[0].shape[0]
    turned[...] = sides[0].T
    for s in range(STREAMS):
        own = pl.multiple_of((2 * s + side[0]) * width, width)
        outs[s][...] = turned[pl.ds(own, width)]


def turned_sides(step, side, sides):
    rows, angles = sides.shape[1:]
    width = angles // UNITS
    return pl.pallas_call(
        turn_kernel,
        grid=(1,),
        out_shape=[jax.ShapeDtypeStruct((width, rows), jnp.bfloat16)] * STREAMS,
        in_specs=[SMEM, pl.BlockSpec((1, rows, angles), lambda i: (step, 0, 0))],
        out_specs=[pl.BlockSpec((width, rows), lambda i: (0, 0))] * STREAMS,
        scratch_shapes=[pltpu.VMEM((angles, rows), jnp.bfloat16)],
        compiler_params=params(),
        cost_estimate=COST,
    )(side, sides)


def wide(value):
    return value.astype(jnp.float32)


def narrow(value):
    return value.astype(jnp.bfloat16)


class Order:
    def __init__(self):
        self.last = None

    def run(self, work, *values):
        if self.last is not None:
            *values, _ = lax.optimization_barrier((*values, self.last))
        result = work(*values)
        self.last = result[0] if isinstance(result, (tuple, list)) else result
        return result

    def block(self, blocks, index):
        self.last = lax.optimization_barrier(self.run(lambda v: v[index], blocks))
        return self.last


def make_per_device(n_row, n_col):
    def trade(value, axis, step):
        size = n_row if axis == "row" else n_col
        return lax.ppermute(value, axis, [(i, i ^ step) for i in range(size)])

    def more_rounds(value, axis):
        size = n_row if axis == "row" else n_col
        step = 4
        while step < size:
            value = value + wide(trade(narrow(value), axis, step))
            step *= 2
        return value

    def per_device(factor_blocks, inverse_blocks, right_sides):
        steps_total, group_rows, angles = right_sides.shape
        last_step = steps_total - 1
        place = lax.axis_index("row")
        core = lax.axis_index("col") & 1
        side = (place & 1) ^ core
        side_ref = side.astype(jnp.int32).reshape(1)
        width = angles // UNITS
        exact = n_row == UNITS
        order = Order()
        solved = [[None] * STREAMS for _ in range(steps_total)]
        state = [dict() for _ in range(STREAMS)]
        sums = [[None] * STREAMS for _ in range(steps_total)]
        factors = [None] * steps_total
        inverses = [None] * steps_total

        def load_factor(step):
            if step < steps_total:
                factors[step] = order.block(factor_blocks, pair_index(step, step - 1))

        def load_inverse(step):
            if step < steps_total:
                inverses[step] = order.block(inverse_blocks, step)

        def older(s, step, blocks):
            if step >= steps_total:
                return
            for j in blocks:
                block = order.block(factor_blocks, pair_index(step, j))
                rest = [] if sums[step][s] is None else [sums[step][s]]
                sums[step][s] = order.run(
                    lambda block, own, other, *rest: product(block, [own, other], rest),
                    block,
                    *solved[j][s],
                    *rest,
                )

        def older_part(s, step, u):
            return [] if sums[step][s] is None else [sums[step][s][u * width : (u + 1) * width]]

        def factor_other(s, step):
            st = state[s]
            leaving = order.run(
                lambda block, x, *rest: product(block, [x], rest, jnp.bfloat16),
                factors[step],
                solved[step - 1][s][1],
                *older_part(s, step, 1),
            )
            st["swap"] = trade(leaving, "col", 1)

        def factor_own(s, step):
            state[s]["sum"] = order.run(
                lambda block, x, *rest: product(block, [x], rest),
                factors[step],
                solved[step - 1][s][0],
                *older_part(s, step, 0),
            )

        def chip_sum(s):
            def work(value, arrived):
                value = value + wide(arrived)
                return narrow(value), value

            st = state[s]
            leaving, st["sum"] = order.run(work, st["sum"], st["swap"])
            st["flight"] = trade(leaving, "col", 2) if n_col > 2 else None

        def residual(s, step):
            def work(side_values, value, *arrived):
                for a in arrived:
                    value = more_rounds(value + wide(a), "col")
                return narrow(wide(side_values) - value)

            st = state[s]
            arrived = [] if st["flight"] is None else [st["flight"]]
            st["own"] = order.run(work, base[s], st["sum"], *arrived)
            st["swap"] = trade(st["own"], "col", 1)

        def inverse_own(s, step):
            st = state[s]
            if exact and step == last_step:
                own, other = st["own"], st["swap"]
                st["own"], st["swap"] = jnp.where(core == 0, other, own), jnp.where(core == 0, own, other)
            leaving = order.run(
                lambda block, x: product(block, [x], kind=jnp.bfloat16), inverses[step], st["own"]
            )
            st["flight"] = trade(leaving, "row", 1)

        def inverse_other(s, step):
            st = state[s]
            st["total"] = order.run(lambda block, x: product(block, [x]), inverses[step], st["swap"])

        def pair_sum(s):
            def work(value, arrived):
                value = value + wide(arrived)
                return narrow(value), value

            st = state[s]
            st["leaving"], st["total"] = order.run(work, st["total"], st["flight"])

        def cross(s):
            st = state[s]
            st["flight"] = trade(st["leaving"], "row", 2) if n_row > 2 else None

        def solve(s, step):
            def work(value, *arrived):
                for a in arrived:
                    value = more_rounds(value + wide(a), "row")
                return narrow(value)

            st = state[s]
            arrived = [] if st["flight"] is None else [st["flight"]]
            other = order.run(work, st["total"], *arrived)
            solved[step][s] = (trade(other, "row", 1), other)

        inverses[0] = order.block(inverse_blocks, 0)
        right = order.block(right_sides, 0)
        def first(s):
            state[s]["total"], leaving = order.run(
                lambda v, w: first_products(s, side_ref, v, w), right, inverses[0]
            )
            state[s]["flight"] = trade(leaving, "row", 1)

        first(0)
        first(1)
        pair_sum(0)
        cross(0)
        load_factor(1)

        for step in range(1, steps_total):
            final = exact and step == last_step
            solve(0, step - 1)
            factor_other(0, step)
            load_inverse(step)
            pair_sum(1)
            cross(1)
            factor_own(0, step)
            chip_sum(0)
            base = order.run(lambda v: turned_sides(step, side_ref, v), right_sides)
            older(1, step, range(step - 1))
            older(0, step + 1, range(step))
            load_factor(step + 1)
            if step == last_step:
                residual(0, step)
            solve(1, step - 1)
            factor_other(1, step)
            if step < last_step:
                residual(0, step)
            inverse_own(0, step)
            factor_own(1, step)
            chip_sum(1)
            inverse_other(0, step)
            pair_sum(0)
            if not final:
                cross(0)
            residual(1, step)
            inverse_own(1, step)
            inverse_other(1, step)
        pair_sum(1)

        outputs = []
        for step in range(steps_total):
            if exact and step == last_step:
                low = place < n_row // 2
                leaving = order.run(
                    lambda a, b: jnp.where(low, b, a), state[0]["leaving"], state[1]["leaving"]
                )
                arrived = trade(leaving, "row", 2)
                found = narrow(jnp.where(low, state[0]["total"], state[1]["total"]) + wide(arrived))
                outputs.append(found.T)
                continue
            if step == last_step:
                solve(0, step)
                cross(1)
                solve(1, step)
            unit = place * UNITS // n_row
            found = solved[step][0][0]
            for s in range(STREAMS):
                for u in range(2):
                    found = jnp.where(unit == 2 * s + (u ^ side), solved[step][s][u], found)
            if not exact:
                slot = angles // n_row
                found = lax.dynamic_slice_in_dim(found, (place * slot) % width, slot, 0)
            outputs.append(found.T)
        return jnp.stack(outputs, axis=0)

    return per_device


def solution(mesh):
    placed = (P("groups", "row", "col"), P("groups", "col", "row"), P("groups", "row", None))
    return jax.shard_map(
        make_per_device(mesh.shape["row"], mesh.shape["col"]),
        mesh=mesh,
        in_specs=placed,
        out_specs=P("groups", "col", "row"),
        check_vma=False,
    )
```

```python
import functools

import jax
import jax.numpy as jnp
from jax import lax
from jax.experimental import pallas as pl
from jax.experimental.pallas import tpu as pltpu
from jax.sharding import PartitionSpec as P

STREAMS = 2
UNITS = 2 * STREAMS


def pair_index(block_row, column_index):
    return block_row * (block_row - 1) // 2 + column_index


VMEM = pl.BlockSpec(memory_space=pltpu.VMEM)
SMEM = pl.BlockSpec(memory_space=pltpu.SMEM)
COST = pl.CostEstimate(flops=1, bytes_accessed=1, transcendentals=0)


def params():
    return pltpu.CompilerParams(vmem_limit_bytes=8 * 2**20)


def times_transposed(left, right):
    return lax.dot_general(left, right, (((1,), (1,)), ((), ())), preferred_element_type=jnp.float32)


TILE = 256


def product_kernel(count, block, *refs):
    units, rest, out = refs[:count], refs[count:-1], refs[-1]
    x = units[0][...] if count == 1 else jnp.concatenate([u[...] for u in units], axis=0)
    rows = block.shape[0]
    tile = min(rows, TILE)
    for t in range(rows // tile):
        cut = pl.ds(t * tile, tile)
        value = times_transposed(block[cut], x).T
        for r in rest:
            value = value + r[:, cut]
        out[:, cut] = value.astype(out.dtype)


def product(block, units, rest=(), kind=jnp.float32):
    angles = sum(u.shape[0] for u in units)
    return pl.pallas_call(
        functools.partial(product_kernel, len(units)),
        out_shape=jax.ShapeDtypeStruct((angles, block.shape[0]), kind),
        in_specs=[VMEM] * (1 + len(units) + len(rest)),
        out_specs=VMEM,
        compiler_params=params(),
        cost_estimate=COST,
    )(block, *units, *rest)


def first_kernel(s, side, right, block, keep, leave, product):
    width = keep.shape[0]
    x = right[:, pl.ds(2 * s * width, 2 * width)].T
    product[...] = times_transposed(x, block[...])
    own = pl.multiple_of(side[0] * width, width)
    other = pl.multiple_of((1 - side[0]) * width, width)
    leave[...] = product[pl.ds(own, width)].astype(jnp.bfloat16)
    keep[...] = product[pl.ds(other, width)]


def first_products(s, side, right, block):
    rows = block.shape[0]
    width = right.shape[1] // UNITS
    return pl.pallas_call(
        functools.partial(first_kernel, s),
        out_shape=(
            jax.ShapeDtypeStruct((width, rows), jnp.float32),
            jax.ShapeDtypeStruct((width, rows), jnp.bfloat16),
        ),
        in_specs=[SMEM, VMEM, VMEM],
        out_specs=(VMEM, VMEM),
        scratch_shapes=[pltpu.VMEM((2 * width, rows), jnp.float32)],
        compiler_params=params(),
        cost_estimate=COST,
    )(side, right, block)


def turn_kernel(width, side, sides, out, turned):
    turned[...] = sides[0].T
    for s in range(STREAMS):
        own = pl.multiple_of((2 * s + side[0]) * width, width)
        out[0, s] = turned[pl.ds(own, width)]


def turned_sides(side, sides):
    steps, rows, angles = sides.shape
    width = angles // UNITS
    return pl.pallas_call(
        functools.partial(turn_kernel, width),
        grid=(steps - 1,),
        out_shape=jax.ShapeDtypeStruct((steps - 1, STREAMS, width, rows), jnp.bfloat16),
        in_specs=[SMEM, pl.BlockSpec((1, rows, angles), lambda i: (i + 1, 0, 0))],
        out_specs=pl.BlockSpec((1, STREAMS, width, rows), lambda i: (i, 0, 0, 0)),
        scratch_shapes=[pltpu.VMEM((angles, rows), jnp.bfloat16)],
        compiler_params=params(),
        cost_estimate=COST,
    )(side, sides)


def wide(value):
    return value.astype(jnp.float32)


def narrow(value):
    return value.astype(jnp.bfloat16)


class Order:
    def __init__(self):
        self.last = None

    def run(self, work, *values):
        if self.last is not None:
            *values, _ = lax.optimization_barrier((*values, self.last))
        result = work(*values)
        self.last = result[0] if isinstance(result, (tuple, list)) else result
        return result

    def block(self, blocks, index):
        self.last = lax.optimization_barrier(self.run(lambda v: v[index], blocks))
        return self.last


def make_per_device(n_row, n_col):
    def trade(value, axis, step):
        size = n_row if axis == "row" else n_col
        return lax.ppermute(value, axis, [(i, i ^ step) for i in range(size)])

    def more_rounds(value, axis):
        size = n_row if axis == "row" else n_col
        step = 4
        while step < size:
            value = value + wide(trade(narrow(value), axis, step))
            step *= 2
        return value

    def per_device(factor_blocks, inverse_blocks, right_sides):
        steps_total, group_rows, angles = right_sides.shape
        last_step = steps_total - 1
        place = lax.axis_index("row")
        core = lax.axis_index("col") & 1
        side = (place & 1) ^ core
        side_ref = side.astype(jnp.int32).reshape(1)
        width = angles // UNITS
        exact = n_row == UNITS
        order = Order()
        solved = [[None] * STREAMS for _ in range(steps_total)]
        state = [dict() for _ in range(STREAMS)]
        sums = [[None] * STREAMS for _ in range(steps_total)]
        factors = [None] * steps_total
        inverses = [None] * steps_total

        def load_factor(step):
            if step < steps_total:
                factors[step] = order.block(factor_blocks, pair_index(step, step - 1))

        def load_inverse(step):
            if step < steps_total:
                inverses[step] = order.block(inverse_blocks, step)

        def older(s, step, blocks):
            if step >= steps_total:
                return
            for j in blocks:
                block = order.block(factor_blocks, pair_index(step, j))
                rest = [] if sums[step][s] is None else [sums[step][s]]
                sums[step][s] = order.run(
                    lambda block, own, other, *rest: product(block, [own, other], rest),
                    block,
                    *solved[j][s],
                    *rest,
                )

        def older_part(s, step, u):
            return [] if sums[step][s] is None else [sums[step][s][u * width : (u + 1) * width]]

        def factor_other(s, step):
            st = state[s]
            leaving = order.run(
                lambda block, x, *rest: product(block, [x], rest, jnp.bfloat16),
                factors[step],
                solved[step - 1][s][1],
                *older_part(s, step, 1),
            )
            st["swap"] = trade(leaving, "col", 1)

        def factor_own(s, step):
            state[s]["sum"] = order.run(
                lambda block, x, *rest: product(block, [x], rest),
                factors[step],
                solved[step - 1][s][0],
                *older_part(s, step, 0),
            )

        def chip_sum(s):
            def work(value, arrived):
                value = value + wide(arrived)
                return narrow(value), value

            st = state[s]
            leaving, st["sum"] = order.run(work, st["sum"], st["swap"])
            st["flight"] = trade(leaving, "col", 2) if n_col > 2 else None

        def residual(s, step):
            def work(side_values, value, *arrived):
                for a in arrived:
                    value = more_rounds(value + wide(a), "col")
                return narrow(wide(side_values) - value)

            st = state[s]
            arrived = [] if st["flight"] is None else [st["flight"]]
            st["own"] = order.run(work, base[step - 1, s], st["sum"], *arrived)
            st["swap"] = trade(st["own"], "col", 1)

        def inverse_own(s, step):
            st = state[s]
            if exact and step == last_step:
                own, other = st["own"], st["swap"]
                st["own"], st["swap"] = jnp.where(core == 0, other, own), jnp.where(core == 0, own, other)
            leaving = order.run(
                lambda block, x: product(block, [x], kind=jnp.bfloat16), inverses[step], st["own"]
            )
            st["flight"] = trade(leaving, "row", 1)

        def inverse_other(s, step):
            st = state[s]
            st["total"] = order.run(lambda block, x: product(block, [x]), inverses[step], st["swap"])

        def pair_sum(s):
            def work(value, arrived):
                value = value + wide(arrived)
                return narrow(value), value

            st = state[s]
            st["leaving"], st["total"] = order.run(work, st["total"], st["flight"])

        def cross(s):
            st = state[s]
            st["flight"] = trade(st["leaving"], "row", 2) if n_row > 2 else None

        def solve(s, step):
            def work(value, *arrived):
                for a in arrived:
                    value = more_rounds(value + wide(a), "row")
                return narrow(value)

            st = state[s]
            arrived = [] if st["flight"] is None else [st["flight"]]
            other = order.run(work, st["total"], *arrived)
            solved[step][s] = (trade(other, "row", 1), other)

        inverses[0] = order.block(inverse_blocks, 0)
        right = order.block(right_sides, 0)
        def first(s):
            state[s]["total"], leaving = order.run(
                lambda v, w: first_products(s, side_ref, v, w), right, inverses[0]
            )
            state[s]["flight"] = trade(leaving, "row", 1)

        first(0)
        first(1)
        if steps_total > 1:
            base = order.run(lambda v: turned_sides(side_ref, v), right_sides)
        pair_sum(0)
        cross(0)
        load_factor(1)
        load_inverse(1)

        for step in range(1, steps_total):
            final = exact and step == last_step
            solve(0, step - 1)
            factor_other(0, step)
            older(1, step, range(step - 1))
            pair_sum(1)
            cross(1)
            factor_own(0, step)
            chip_sum(0)
            older(0, step + 1, range(step))
            load_factor(step + 1)
            load_inverse(step + 1)
            if step == last_step:
                residual(0, step)
                solve(1, step - 1)
                factor_other(1, step)
            else:
                solve(1, step - 1)
                factor_other(1, step)
                residual(0, step)
            inverse_own(0, step)
            factor_own(1, step)
            chip_sum(1)
            inverse_other(0, step)
            pair_sum(0)
            if not final:
                cross(0)
            residual(1, step)
            inverse_own(1, step)
            inverse_other(1, step)
        pair_sum(1)

        outputs = []
        for step in range(steps_total):
            if exact and step == last_step:
                low = place < n_row // 2
                leaving = order.run(
                    lambda a, b: jnp.where(low, b, a), state[0]["leaving"], state[1]["leaving"]
                )
                arrived = trade(leaving, "row", 2)
                found = narrow(jnp.where(low, state[0]["total"], state[1]["total"]) + wide(arrived))
                outputs.append(found.T)
                continue
            if step == last_step:
                solve(0, step)
                cross(1)
                solve(1, step)
            unit = place * UNITS // n_row
            found = solved[step][0][0]
            for s in range(STREAMS):
                for u in range(2):
                    found = jnp.where(unit == 2 * s + (u ^ side), solved[step][s][u], found)
            if not exact:
                slot = angles // n_row
                found = lax.dynamic_slice_in_dim(found, (place * slot) % width, slot, 0)
            outputs.append(found.T)
        return jnp.stack(outputs, axis=0)

    return per_device


def solution(mesh):
    placed = (P("groups", "row", "col"), P("groups", "col", "row"), P("groups", "row", None))
    return jax.shard_map(
        make_per_device(mesh.shape["row"], mesh.shape["col"]),
        mesh=mesh,
        in_specs=placed,
        out_specs=P("groups", "col", "row"),
        check_vma=False,
    )
```

```python
import functools

import jax
import jax.numpy as jnp
from jax import lax
from jax.experimental import pallas as pl
from jax.experimental.pallas import tpu as pltpu
from jax.sharding import PartitionSpec as P

STREAMS = 2
UNITS = 2 * STREAMS


def pair_index(block_row, column_index):
    return block_row * (block_row - 1) // 2 + column_index


VMEM = pl.BlockSpec(memory_space=pltpu.VMEM)
SMEM = pl.BlockSpec(memory_space=pltpu.SMEM)
COST = pl.CostEstimate(flops=1, bytes_accessed=1, transcendentals=0)


def params():
    return pltpu.CompilerParams(vmem_limit_bytes=8 * 2**20)


def times_transposed(left, right):
    return lax.dot_general(left, right, (((1,), (1,)), ((), ())), preferred_element_type=jnp.float32)


TILE = 256


def product_kernel(count, block, *refs):
    units, rest, out = refs[:count], refs[count:-1], refs[-1]
    x = units[0][...] if count == 1 else jnp.concatenate([u[...] for u in units], axis=0)
    rows = block.shape[0]
    tile = min(rows, TILE)
    for t in range(rows // tile):
        cut = pl.ds(t * tile, tile)
        value = times_transposed(block[cut], x).T
        for r in rest:
            value = value + r[:, cut]
        out[:, cut] = value.astype(out.dtype)


def product(block, units, rest=(), kind=jnp.float32):
    angles = sum(u.shape[0] for u in units)
    return pl.pallas_call(
        functools.partial(product_kernel, len(units)),
        out_shape=jax.ShapeDtypeStruct((angles, block.shape[0]), kind),
        in_specs=[VMEM] * (1 + len(units) + len(rest)),
        out_specs=VMEM,
        compiler_params=params(),
        cost_estimate=COST,
    )(block, *units, *rest)


def first_kernel(s, side, right, block, keep, leave, product):
    width = keep.shape[0]
    x = right[:, pl.ds(2 * s * width, 2 * width)].T
    product[...] = times_transposed(x, block[...])
    own = pl.multiple_of(side[0] * width, width)
    other = pl.multiple_of((1 - side[0]) * width, width)
    leave[...] = product[pl.ds(own, width)].astype(jnp.bfloat16)
    keep[...] = product[pl.ds(other, width)]


def first_products(s, side, right, block):
    rows = block.shape[0]
    width = right.shape[1] // UNITS
    return pl.pallas_call(
        functools.partial(first_kernel, s),
        out_shape=(
            jax.ShapeDtypeStruct((width, rows), jnp.float32),
            jax.ShapeDtypeStruct((width, rows), jnp.bfloat16),
        ),
        in_specs=[SMEM, VMEM, VMEM],
        out_specs=(VMEM, VMEM),
        scratch_shapes=[pltpu.VMEM((2 * width, rows), jnp.float32)],
        compiler_params=params(),
        cost_estimate=COST,
    )(side, right, block)


def turn_kernel(width, side, sides, out, turned):
    turned[...] = sides[0].T
    for s in range(STREAMS):
        own = pl.multiple_of((2 * s + side[0]) * width, width)
        out[0, s] = turned[pl.ds(own, width)]


def turned_sides(side, sides):
    steps, rows, angles = sides.shape
    width = angles // UNITS
    return pl.pallas_call(
        functools.partial(turn_kernel, width),
        grid=(steps - 1,),
        out_shape=jax.ShapeDtypeStruct((steps - 1, STREAMS, width, rows), jnp.bfloat16),
        in_specs=[SMEM, pl.BlockSpec((1, rows, angles), lambda i: (i + 1, 0, 0))],
        out_specs=pl.BlockSpec((1, STREAMS, width, rows), lambda i: (i, 0, 0, 0)),
        scratch_shapes=[pltpu.VMEM((angles, rows), jnp.bfloat16)],
        compiler_params=params(),
        cost_estimate=COST,
    )(side, sides)


def wide(value):
    return value.astype(jnp.float32)


def narrow(value):
    return value.astype(jnp.bfloat16)


class Order:
    def __init__(self):
        self.last = None

    def run(self, work, *values):
        if self.last is not None:
            *values, _ = lax.optimization_barrier((*values, self.last))
        result = work(*values)
        self.last = result[0] if isinstance(result, (tuple, list)) else result
        return result

    def block(self, blocks, index):
        self.last = lax.optimization_barrier(self.run(lambda v: v[index], blocks))
        return self.last


def make_per_device(n_row, n_col):
    def trade(value, axis, step):
        size = n_row if axis == "row" else n_col
        return lax.ppermute(value, axis, [(i, i ^ step) for i in range(size)])

    def more_rounds(value, axis):
        size = n_row if axis == "row" else n_col
        step = 4
        while step < size:
            value = value + wide(trade(narrow(value), axis, step))
            step *= 2
        return value

    def per_device(factor_blocks, inverse_blocks, right_sides):
        steps_total, group_rows, angles = right_sides.shape
        last_step = steps_total - 1
        place = lax.axis_index("row")
        core = lax.axis_index("col") & 1
        side = (place & 1) ^ core
        side_ref = side.astype(jnp.int32).reshape(1)
        width = angles // UNITS
        exact = n_row == UNITS
        order = Order()
        solved = [[None] * STREAMS for _ in range(steps_total)]
        state = [dict() for _ in range(STREAMS)]
        sums = [None] * (steps_total + 1)
        factors = [None] * steps_total
        inverses = [None] * steps_total

        def load_factor(step):
            if step < steps_total:
                factors[step] = order.block(factor_blocks, pair_index(step, step - 1))

        def load_inverse(step):
            if step < steps_total:
                inverses[step] = order.block(inverse_blocks, step)

        def older(step, blocks):
            if step >= steps_total:
                return
            for j in blocks:
                block = order.block(factor_blocks, pair_index(step, j))
                units = [u for s in range(STREAMS) for u in solved[j][s]]

                rest = [] if sums[step] is None else [sums[step]]
                sums[step] = order.run(
                    lambda block, *v: product(block, v[: len(units)], v[len(units) :]), block, *units, *rest
                )

        def older_part(s, step, u):
            first = (2 * s + u) * width
            return [] if sums[step] is None else [sums[step][first : first + width]]

        def factor_other(s, step):
            st = state[s]
            leaving = order.run(
                lambda block, x, *rest: product(block, [x], rest, jnp.bfloat16),
                factors[step],
                solved[step - 1][s][1],
                *older_part(s, step, 1),
            )
            st["swap"] = trade(leaving, "col", 1)

        def factor_own(s, step):
            state[s]["sum"] = order.run(
                lambda block, x, *rest: product(block, [x], rest),
                factors[step],
                solved[step - 1][s][0],
                *older_part(s, step, 0),
            )

        def chip_sum(s):
            def work(value, arrived):
                value = value + wide(arrived)
                return narrow(value), value

            st = state[s]
            leaving, st["sum"] = order.run(work, st["sum"], st["swap"])
            st["flight"] = trade(leaving, "col", 2) if n_col > 2 else None

        def residual(s, step):
            def work(side_values, value, *arrived):
                for a in arrived:
                    value = more_rounds(value + wide(a), "col")
                return narrow(wide(side_values) - value)

            st = state[s]
            arrived = [] if st["flight"] is None else [st["flight"]]
            st["own"] = order.run(work, base[step - 1, s], st["sum"], *arrived)
            st["swap"] = trade(st["own"], "col", 1)

        def inverse_own(s, step):
            st = state[s]
            if exact and step == last_step:
                own, other = st["own"], st["swap"]
                st["own"], st["swap"] = jnp.where(core == 0, other, own), jnp.where(core == 0, own, other)
            leaving = order.run(
                lambda block, x: product(block, [x], kind=jnp.bfloat16), inverses[step], st["own"]
            )
            st["flight"] = trade(leaving, "row", 1)

        def inverse_other(s, step):
            st = state[s]
            st["total"] = order.run(lambda block, x: product(block, [x]), inverses[step], st["swap"])

        def pair_sum(s):
            def work(value, arrived):
                value = value + wide(arrived)
                return narrow(value), value

            st = state[s]
            st["leaving"], st["total"] = order.run(work, st["total"], st["flight"])

        def cross(s):
            st = state[s]
            st["flight"] = trade(st["leaving"], "row", 2) if n_row > 2 else None

        def solve(s, step):
            def work(value, *arrived):
                for a in arrived:
                    value = more_rounds(value + wide(a), "row")
                return narrow(value)

            st = state[s]
            arrived = [] if st["flight"] is None else [st["flight"]]
            other = order.run(work, st["total"], *arrived)
            solved[step][s] = (trade(other, "row", 1), other)

        inverses[0] = order.block(inverse_blocks, 0)
        right = order.block(right_sides, 0)
        def first(s):
            state[s]["total"], leaving = order.run(
                lambda v, w: first_products(s, side_ref, v, w), right, inverses[0]
            )
            state[s]["flight"] = trade(leaving, "row", 1)

        first(0)
        first(1)
        if steps_total > 1:
            base = order.run(lambda v: turned_sides(side_ref, v), right_sides)
        pair_sum(0)
        cross(0)
        load_factor(1)

        for step in range(1, steps_total):
            final = exact and step == last_step
            solve(0, step - 1)
            factor_other(0, step)
            pair_sum(1)
            cross(1)
            factor_own(0, step)
            chip_sum(0)
            older(step + 1, range(step - 1))
            load_factor(step + 1)
            load_inverse(step)
            if final:
                residual(0, step)
                solve(1, step - 1)
                factor_other(1, step)
                factor_own(1, step)
                chip_sum(1)
                inverse_own(0, step)
                inverse_other(0, step)
                residual(1, step)
                pair_sum(0)
                inverse_own(1, step)
                inverse_other(1, step)
                continue
            solve(1, step - 1)
            factor_other(1, step)
            residual(0, step)
            inverse_own(0, step)
            factor_own(1, step)
            chip_sum(1)
            older(step + 1, [step - 1])
            inverse_other(0, step)
            pair_sum(0)
            cross(0)
            residual(1, step)
            inverse_own(1, step)
            inverse_other(1, step)
        pair_sum(1)

        outputs = []
        for step in range(steps_total):
            if exact and step == last_step:
                low = place < n_row // 2
                leaving = order.run(
                    lambda a, b: jnp.where(low, b, a), state[0]["leaving"], state[1]["leaving"]
                )
                arrived = trade(leaving, "row", 2)
                found = narrow(jnp.where(low, state[0]["total"], state[1]["total"]) + wide(arrived))
                outputs.append(found.T)
                continue
            if step == last_step:
                solve(0, step)
                cross(1)
                solve(1, step)
            unit = place * UNITS // n_row
            found = solved[step][0][0]
            for s in range(STREAMS):
                for u in range(2):
                    found = jnp.where(unit == 2 * s + (u ^ side), solved[step][s][u], found)
            if not exact:
                slot = angles // n_row
                found = lax.dynamic_slice_in_dim(found, (place * slot) % width, slot, 0)
            outputs.append(found.T)
        return jnp.stack(outputs, axis=0)

    return per_device


def solution(mesh):
    placed = (P("groups", "row", "col"), P("groups", "col", "row"), P("groups", "row", None))
    return jax.shard_map(
        make_per_device(mesh.shape["row"], mesh.shape["col"]),
        mesh=mesh,
        in_specs=placed,
        out_specs=P("groups", "col", "row"),
        check_vma=False,
    )
```

```python
import functools

import jax
import jax.numpy as jnp
from jax import lax
from jax.experimental import pallas as pl
from jax.experimental.pallas import tpu as pltpu
from jax.sharding import PartitionSpec as P

STREAMS = 2
UNITS = 2 * STREAMS


def pair_index(block_row, column_index):
    return block_row * (block_row - 1) // 2 + column_index


VMEM = pl.BlockSpec(memory_space=pltpu.VMEM)
SMEM = pl.BlockSpec(memory_space=pltpu.SMEM)
COST = pl.CostEstimate(flops=1, bytes_accessed=1, transcendentals=0)


def params():
    return pltpu.CompilerParams(vmem_limit_bytes=8 * 2**20)


def times_transposed(left, right):
    return lax.dot_general(left, right, (((1,), (1,)), ((), ())), preferred_element_type=jnp.float32)


TILE = 256


def product_kernel(count, block, *refs):
    units, rest, out = refs[:count], refs[count:-1], refs[-1]
    x = units[0][...] if count == 1 else jnp.concatenate([u[...] for u in units], axis=0)
    rows = block.shape[0]
    tile = min(rows, TILE)
    for t in range(rows // tile):
        cut = pl.ds(t * tile, tile)
        value = times_transposed(block[cut], x).T
        for r in rest:
            value = value + r[:, cut]
        out[:, cut] = value.astype(out.dtype)


def product(block, units, rest=(), kind=jnp.float32):
    angles = sum(u.shape[0] for u in units)
    return pl.pallas_call(
        functools.partial(product_kernel, len(units)),
        out_shape=jax.ShapeDtypeStruct((angles, block.shape[0]), kind),
        in_specs=[VMEM] * (1 + len(units) + len(rest)),
        out_specs=VMEM,
        compiler_params=params(),
        cost_estimate=COST,
    )(block, *units, *rest)


def first_kernel(s, side, right, block, keep, leave, product):
    width = keep.shape[0]
    x = right[...].T
    x = jnp.concatenate(
        [x[g * width : (g + 1) * width] for g in (s, STREAMS + s)], axis=0
    )
    product[...] = times_transposed(x, block[...])
    own = pl.multiple_of(side[0] * width, width)
    other = pl.multiple_of((1 - side[0]) * width, width)
    leave[...] = product[pl.ds(own, width)].astype(jnp.bfloat16)
    keep[...] = product[pl.ds(other, width)]


def first_products(s, side, right, block):
    rows = block.shape[0]
    width = right.shape[1] // UNITS
    return pl.pallas_call(
        functools.partial(first_kernel, s),
        out_shape=(
            jax.ShapeDtypeStruct((width, rows), jnp.float32),
            jax.ShapeDtypeStruct((width, rows), jnp.bfloat16),
        ),
        in_specs=[SMEM, VMEM, VMEM],
        out_specs=(VMEM, VMEM),
        scratch_shapes=[pltpu.VMEM((2 * width, rows), jnp.float32)],
        compiler_params=params(),
        cost_estimate=COST,
    )(side, right, block)


def turn_kernel(width, side, sides, out, turned):
    turned[...] = sides[0].T
    for s in range(STREAMS):
        own = pl.multiple_of((STREAMS * side[0] + s) * width, width)
        out[0, s] = turned[pl.ds(own, width)]


def turned_sides(side, sides):
    steps, rows, angles = sides.shape
    width = angles // UNITS
    return pl.pallas_call(
        functools.partial(turn_kernel, width),
        grid=(steps - 1,),
        out_shape=jax.ShapeDtypeStruct((steps - 1, STREAMS, width, rows), jnp.bfloat16),
        in_specs=[SMEM, pl.BlockSpec((1, rows, angles), lambda i: (i + 1, 0, 0))],
        out_specs=pl.BlockSpec((1, STREAMS, width, rows), lambda i: (i, 0, 0, 0)),
        scratch_shapes=[pltpu.VMEM((angles, rows), jnp.bfloat16)],
        compiler_params=params(),
        cost_estimate=COST,
    )(side, sides)


def wide(value):
    return value.astype(jnp.float32)


def narrow(value):
    return value.astype(jnp.bfloat16)


class Order:
    def __init__(self):
        self.last = None

    def run(self, work, *values):
        if self.last is not None:
            *values, _ = lax.optimization_barrier((*values, self.last))
        result = work(*values)
        self.last = result[0] if isinstance(result, (tuple, list)) else result
        return result

    def block(self, blocks, index):
        self.last = lax.optimization_barrier(self.run(lambda v: v[index], blocks))
        return self.last


def make_per_device(n_row, n_col):
    def trade(value, axis, step):
        size = n_row if axis == "row" else n_col
        return lax.ppermute(value, axis, [(i, i ^ step) for i in range(size)])

    def more_rounds(value, axis):
        size = n_row if axis == "row" else n_col
        step = 4
        while step < size:
            value = value + wide(trade(narrow(value), axis, step))
            step *= 2
        return value

    def per_device(factor_blocks, inverse_blocks, right_sides):
        steps_total, group_rows, angles = right_sides.shape
        last_step = steps_total - 1
        place = lax.axis_index("row")
        core = lax.axis_index("col") & 1
        side = (place & 1) ^ core
        side_ref = side.astype(jnp.int32).reshape(1)
        width = angles // UNITS
        exact = n_row == UNITS
        order = Order()
        solved = [[None] * STREAMS for _ in range(steps_total)]
        state = [dict() for _ in range(STREAMS)]
        sums = [None] * (steps_total + 1)
        factors = [None] * steps_total
        inverses = [None] * steps_total

        def load_factor(step):
            if step < steps_total:
                factors[step] = order.block(factor_blocks, pair_index(step, step - 1))

        def load_inverse(step):
            if step < steps_total:
                inverses[step] = order.block(inverse_blocks, step)

        def older(step, blocks):
            if step >= steps_total:
                return
            for j in blocks:
                block = order.block(factor_blocks, pair_index(step, j))
                units = [u for s in range(STREAMS) for u in solved[j][s]]

                rest = [] if sums[step] is None else [sums[step]]
                sums[step] = order.run(
                    lambda block, *v: product(block, v[: len(units)], v[len(units) :]), block, *units, *rest
                )

        def older_part(s, step, u):
            first = (2 * s + u) * width
            return [] if sums[step] is None else [sums[step][first : first + width]]

        def factor_other(s, step):
            st = state[s]
            leaving = order.run(
                lambda block, x, *rest: product(block, [x], rest, jnp.bfloat16),
                factors[step],
                solved[step - 1][s][1],
                *older_part(s, step, 1),
            )
            st["swap"] = trade(leaving, "col", 1)

        def factor_own(s, step):
            state[s]["sum"] = order.run(
                lambda block, x, *rest: product(block, [x], rest),
                factors[step],
                solved[step - 1][s][0],
                *older_part(s, step, 0),
            )

        def chip_sum(s):
            def work(value, arrived):
                value = value + wide(arrived)
                return narrow(value), value

            st = state[s]
            leaving, st["sum"] = order.run(work, st["sum"], st["swap"])
            st["flight"] = trade(leaving, "col", 2) if n_col > 2 else None

        def residual(s, step):
            def work(side_values, value, *arrived):
                for a in arrived:
                    value = more_rounds(value + wide(a), "col")
                return narrow(wide(side_values) - value)

            st = state[s]
            arrived = [] if st["flight"] is None else [st["flight"]]
            st["own"] = order.run(work, base[step - 1, s], st["sum"], *arrived)
            st["swap"] = trade(st["own"], "col", 1)

        def inverse_own(s, step):
            st = state[s]
            if exact and step == last_step:
                own, other = st["own"], st["swap"]
                stays = core == (s ^ (place >> 1))
                st["own"], st["swap"] = jnp.where(stays, other, own), jnp.where(stays, own, other)
            leaving = order.run(
                lambda block, x: product(block, [x], kind=jnp.bfloat16), inverses[step], st["own"]
            )
            st["flight"] = trade(leaving, "row", 1)

        def inverse_other(s, step):
            st = state[s]
            st["total"] = order.run(lambda block, x: product(block, [x]), inverses[step], st["swap"])

        def pair_sum(s):
            def work(value, arrived):
                value = value + wide(arrived)
                return narrow(value), value

            st = state[s]
            st["leaving"], st["total"] = order.run(work, st["total"], st["flight"])

        def cross(s):
            st = state[s]
            st["flight"] = trade(st["leaving"], "row", 2) if n_row > 2 else None

        def final_cross(s):
            st = state[s]
            pairs = [(r ^ (n_row - 1), r) for r in range(n_row) if r % STREAMS == s]
            st["flight"] = lax.ppermute(st["leaving"], "row", pairs)

        def solve(s, step):
            def work(value, *arrived):
                for a in arrived:
                    value = more_rounds(value + wide(a), "row")
                return narrow(value)

            st = state[s]
            arrived = [] if st["flight"] is None else [st["flight"]]
            other = order.run(work, st["total"], *arrived)
            solved[step][s] = (trade(other, "row", 1), other)

        inverses[0] = order.block(inverse_blocks, 0)
        right = order.block(right_sides, 0)
        def first(s):
            state[s]["total"], leaving = order.run(
                lambda v, w: first_products(s, side_ref, v, w), right, inverses[0]
            )
            state[s]["flight"] = trade(leaving, "row", 1)

        first(0)
        first(1)
        if steps_total > 1:
            base = order.run(lambda v: turned_sides(side_ref, v), right_sides)
        pair_sum(0)
        cross(0)
        load_factor(1)

        for step in range(1, steps_total):
            final = exact and step == last_step
            solve(0, step - 1)
            factor_other(0, step)
            pair_sum(1)
            cross(1)
            factor_own(0, step)
            chip_sum(0)
            older(step + 1, range(step - 1))
            load_factor(step + 1)
            load_inverse(step)
            if final:
                residual(0, step)
                solve(1, step - 1)
                factor_other(1, step)
                factor_own(1, step)
                chip_sum(1)
                inverse_own(0, step)
                inverse_other(0, step)
                residual(1, step)
                pair_sum(0)
                final_cross(0)
                inverse_own(1, step)
                inverse_other(1, step)
                continue
            solve(1, step - 1)
            factor_other(1, step)
            residual(0, step)
            inverse_own(0, step)
            factor_own(1, step)
            chip_sum(1)
            older(step + 1, [step - 1])
            inverse_other(0, step)
            pair_sum(0)
            cross(0)
            residual(1, step)
            inverse_own(1, step)
            inverse_other(1, step)
        pair_sum(1)

        outputs = []
        for step in range(steps_total):
            if exact and step == last_step:
                final_cross(1)
                even = (place & 1) == 0
                found = jnp.where(even, state[0]["total"], state[1]["total"])
                found = found + wide(jnp.where(even, state[0]["flight"], state[1]["flight"]))
                found = narrow(found)
                outputs.append(found.T)
                continue
            if step == last_step:
                solve(0, step)
                cross(1)
                solve(1, step)
            unit = place * UNITS // n_row
            found = solved[step][0][0]
            for s in range(STREAMS):
                for u in range(2):
                    found = jnp.where(unit == STREAMS * (u ^ side) + s, solved[step][s][u], found)
            if not exact:
                slot = angles // n_row
                found = lax.dynamic_slice_in_dim(found, (place * slot) % width, slot, 0)
            outputs.append(found.T)
        return jnp.stack(outputs, axis=0)

    return per_device


def solution(mesh):
    placed = (P("groups", "row", "col"), P("groups", "col", "row"), P("groups", "row", None))
    return jax.shard_map(
        make_per_device(mesh.shape["row"], mesh.shape["col"]),
        mesh=mesh,
        in_specs=placed,
        out_specs=P("groups", "col", "row"),
        check_vma=False,
    )
```

```python
import functools

import jax
import jax.numpy as jnp
from jax import lax
from jax.experimental import pallas as pl
from jax.experimental.pallas import tpu as pltpu
from jax.sharding import PartitionSpec as P

STREAMS = 2
UNITS = 2 * STREAMS


def pair_index(block_row, column_index):
    return block_row * (block_row - 1) // 2 + column_index


VMEM = pl.BlockSpec(memory_space=pltpu.VMEM)
SMEM = pl.BlockSpec(memory_space=pltpu.SMEM)
COST = pl.CostEstimate(flops=1, bytes_accessed=1, transcendentals=0)


def params():
    return pltpu.CompilerParams(vmem_limit_bytes=8 * 2**20)


def times_transposed(left, right):
    return lax.dot_general(left, right, (((1,), (1,)), ((), ())), preferred_element_type=jnp.float32)


TILE = 256


def product_kernel(count, block, *refs):
    units, rest, out = refs[:count], refs[count:-1], refs[-1]
    x = units[0][...] if count == 1 else jnp.concatenate([u[...] for u in units], axis=0)
    rows = block.shape[0]
    tile = min(rows, TILE)
    for t in range(rows // tile):
        cut = pl.ds(t * tile, tile)
        value = times_transposed(block[cut], x).T
        for r in rest:
            value = value + r[:, cut]
        out[:, cut] = value.astype(out.dtype)


def product(block, units, rest=(), kind=jnp.float32):
    angles = sum(u.shape[0] for u in units)
    return pl.pallas_call(
        functools.partial(product_kernel, len(units)),
        out_shape=jax.ShapeDtypeStruct((angles, block.shape[0]), kind),
        in_specs=[VMEM] * (1 + len(units) + len(rest)),
        out_specs=VMEM,
        compiler_params=params(),
        cost_estimate=COST,
    )(block, *units, *rest)


def first_kernel(s, side, right, block, keep, leave, product):
    width = keep.shape[0]
    x = right[...].T
    x = jnp.concatenate(
        [x[unit_place(s, h) * width : (unit_place(s, h) + 1) * width] for h in range(2)], axis=0
    )
    product[...] = times_transposed(x, block[...])
    own = pl.multiple_of(side[0] * width, width)
    other = pl.multiple_of((1 - side[0]) * width, width)
    leave[...] = product[pl.ds(own, width)].astype(jnp.bfloat16)
    keep[...] = product[pl.ds(other, width)]


def first_products(s, side, right, block):
    rows = block.shape[0]
    width = right.shape[1] // UNITS
    return pl.pallas_call(
        functools.partial(first_kernel, s),
        out_shape=(
            jax.ShapeDtypeStruct((width, rows), jnp.float32),
            jax.ShapeDtypeStruct((width, rows), jnp.bfloat16),
        ),
        in_specs=[SMEM, VMEM, VMEM],
        out_specs=(VMEM, VMEM),
        scratch_shapes=[pltpu.VMEM((2 * width, rows), jnp.float32)],
        compiler_params=params(),
        cost_estimate=COST,
    )(side, right, block)


def turn_kernel(width, side, sides, out, turned):
    turned[...] = sides[0].T
    for s in range(STREAMS):
        own = pl.multiple_of(unit_place(s, side[0]) * width, width)
        out[0, s] = turned[pl.ds(own, width)]


def turned_sides(side, sides):
    steps, rows, angles = sides.shape
    width = angles // UNITS
    return pl.pallas_call(
        functools.partial(turn_kernel, width),
        grid=(steps - 1,),
        out_shape=jax.ShapeDtypeStruct((steps - 1, STREAMS, width, rows), jnp.bfloat16),
        in_specs=[SMEM, pl.BlockSpec((1, rows, angles), lambda i: (i + 1, 0, 0))],
        out_specs=pl.BlockSpec((1, STREAMS, width, rows), lambda i: (i, 0, 0, 0)),
        scratch_shapes=[pltpu.VMEM((angles, rows), jnp.bfloat16)],
        compiler_params=params(),
        cost_estimate=COST,
    )(side, sides)


def wide(value):
    return value.astype(jnp.float32)


def narrow(value):
    return value.astype(jnp.bfloat16)


def unit_place(s, h):
    return STREAMS * h + (h if s == 0 else 1 - h)


class Order:
    def __init__(self):
        self.last = None

    def run(self, work, *values):
        if self.last is not None:
            *values, _ = lax.optimization_barrier((*values, self.last))
        result = work(*values)
        self.last = result[0] if isinstance(result, (tuple, list)) else result
        return result

    def block(self, blocks, index):
        self.last = lax.optimization_barrier(self.run(lambda v: v[index], blocks))
        return self.last


def make_per_device(n_row, n_col):
    def trade(value, axis, step):
        size = n_row if axis == "row" else n_col
        return lax.ppermute(value, axis, [(i, i ^ step) for i in range(size)])

    def more_rounds(value, axis):
        size = n_row if axis == "row" else n_col
        step = 4
        while step < size:
            value = value + wide(trade(narrow(value), axis, step))
            step *= 2
        return value

    def per_device(factor_blocks, inverse_blocks, right_sides):
        steps_total, group_rows, angles = right_sides.shape
        last_step = steps_total - 1
        place = lax.axis_index("row")
        core = lax.axis_index("col") & 1
        side = (place & 1) ^ core
        side_ref = side.astype(jnp.int32).reshape(1)
        width = angles // UNITS
        exact = n_row == UNITS
        order = Order()
        solved = [[None] * STREAMS for _ in range(steps_total)]
        state = [dict() for _ in range(STREAMS)]
        sums = [None] * (steps_total + 1)
        factors = [None] * steps_total
        inverses = [None] * steps_total

        def load_factor(step):
            if step < steps_total:
                factors[step] = order.block(factor_blocks, pair_index(step, step - 1))

        def load_inverse(step):
            if step < steps_total:
                inverses[step] = order.block(inverse_blocks, step)

        def older(step, blocks):
            if step >= steps_total:
                return
            for j in blocks:
                block = order.block(factor_blocks, pair_index(step, j))
                units = [u for s in range(STREAMS) for u in solved[j][s]]

                rest = [] if sums[step] is None else [sums[step]]
                sums[step] = order.run(
                    lambda block, *v: product(block, v[: len(units)], v[len(units) :]), block, *units, *rest
                )

        def older_part(s, step, u):
            first = (2 * s + u) * width
            return [] if sums[step] is None else [sums[step][first : first + width]]

        def factor_other(s, step):
            st = state[s]
            leaving = order.run(
                lambda block, x, *rest: product(block, [x], rest, jnp.bfloat16),
                factors[step],
                solved[step - 1][s][1],
                *older_part(s, step, 1),
            )
            st["swap"] = trade(leaving, "col", 1)

        def factor_own(s, step):
            state[s]["sum"] = order.run(
                lambda block, x, *rest: product(block, [x], rest),
                factors[step],
                solved[step - 1][s][0],
                *older_part(s, step, 0),
            )

        def chip_sum(s):
            def work(value, arrived):
                value = value + wide(arrived)
                return narrow(value), value

            st = state[s]
            leaving, st["sum"] = order.run(work, st["sum"], st["swap"])
            st["flight"] = trade(leaving, "col", 2) if n_col > 2 else None

        def residual(s, step):
            def work(side_values, value, *arrived):
                for a in arrived:
                    value = more_rounds(value + wide(a), "col")
                return narrow(wide(side_values) - value)

            st = state[s]
            arrived = [] if st["flight"] is None else [st["flight"]]
            st["own"] = order.run(work, base[step - 1, s], st["sum"], *arrived)
            st["swap"] = trade(st["own"], "col", 1)

        def inverse_own(s, step):
            st = state[s]
            if exact and step == last_step:
                own, other = st["own"], st["swap"]
                stays = core == s
                st["own"], st["swap"] = jnp.where(stays, other, own), jnp.where(stays, own, other)
            leaving = order.run(
                lambda block, x: product(block, [x], kind=jnp.bfloat16), inverses[step], st["own"]
            )
            st["flight"] = trade(leaving, "row", 1)

        def inverse_other(s, step):
            st = state[s]
            st["total"] = order.run(lambda block, x: product(block, [x]), inverses[step], st["swap"])

        def pair_sum(s):
            def work(value, arrived):
                value = value + wide(arrived)
                return narrow(value), value

            st = state[s]
            st["leaving"], st["total"] = order.run(work, st["total"], st["flight"])

        def cross(s):
            st = state[s]
            st["flight"] = trade(st["leaving"], "row", 2) if n_row > 2 else None

        def final_cross(s):
            st = state[s]
            pairs = [(r ^ 2, r) for r in range(n_row) if r in [unit_place(s, h) for h in range(2)]]
            st["flight"] = lax.ppermute(st["leaving"], "row", pairs)

        def solve(s, step):
            def work(value, *arrived):
                for a in arrived:
                    value = more_rounds(value + wide(a), "row")
                return narrow(value)

            st = state[s]
            arrived = [] if st["flight"] is None else [st["flight"]]
            other = order.run(work, st["total"], *arrived)
            solved[step][s] = (trade(other, "row", 1), other)

        inverses[0] = order.block(inverse_blocks, 0)
        right = order.block(right_sides, 0)
        def first(s):
            state[s]["total"], leaving = order.run(
                lambda v, w: first_products(s, side_ref, v, w), right, inverses[0]
            )
            state[s]["flight"] = trade(leaving, "row", 1)

        first(0)
        first(1)
        if steps_total > 1:
            base = order.run(lambda v: turned_sides(side_ref, v), right_sides)
        pair_sum(0)
        cross(0)
        load_factor(1)

        for step in range(1, steps_total):
            final = exact and step == last_step
            solve(0, step - 1)
            factor_other(0, step)
            pair_sum(1)
            cross(1)
            factor_own(0, step)
            chip_sum(0)
            older(step + 1, range(step - 1))
            load_factor(step + 1)
            load_inverse(step)
            if final:
                residual(0, step)
                solve(1, step - 1)
                factor_other(1, step)
                factor_own(1, step)
                chip_sum(1)
                inverse_own(0, step)
                inverse_other(0, step)
                residual(1, step)
                pair_sum(0)
                final_cross(0)
                inverse_own(1, step)
                inverse_other(1, step)
                continue
            solve(1, step - 1)
            factor_other(1, step)
            residual(0, step)
            inverse_own(0, step)
            factor_own(1, step)
            chip_sum(1)
            older(step + 1, [step - 1])
            inverse_other(0, step)
            pair_sum(0)
            cross(0)
            residual(1, step)
            inverse_own(1, step)
            inverse_other(1, step)
        pair_sum(1)

        outputs = []
        for step in range(steps_total):
            if exact and step == last_step:
                final_cross(1)
                first_gives = ((place ^ (place >> 1)) & 1) == 0
                found = jnp.where(first_gives, state[0]["total"], state[1]["total"])
                found = found + wide(jnp.where(first_gives, state[0]["flight"], state[1]["flight"]))
                found = narrow(found)
                outputs.append(found.T)
                continue
            if step == last_step:
                solve(0, step)
                cross(1)
                solve(1, step)
            unit = place * UNITS // n_row
            found = solved[step][0][0]
            for s in range(STREAMS):
                for u in range(2):
                    found = jnp.where(unit == unit_place(s, u ^ side), solved[step][s][u], found)
            if not exact:
                slot = angles // n_row
                found = lax.dynamic_slice_in_dim(found, (place * slot) % width, slot, 0)
            outputs.append(found.T)
        return jnp.stack(outputs, axis=0)

    return per_device


def solution(mesh):
    placed = (P("groups", "row", "col"), P("groups", "col", "row"), P("groups", "row", None))
    return jax.shard_map(
        make_per_device(mesh.shape["row"], mesh.shape["col"]),
        mesh=mesh,
        in_specs=placed,
        out_specs=P("groups", "col", "row"),
        check_vma=False,
    )
```

```python
import functools

import jax
import jax.numpy as jnp
from jax import lax
from jax.experimental import pallas as pl
from jax.experimental.pallas import tpu as pltpu
from jax.sharding import PartitionSpec as P

STREAMS = 2
UNITS = 2 * STREAMS


def pair_index(block_row, column_index):
    return block_row * (block_row - 1) // 2 + column_index


VMEM = pl.BlockSpec(memory_space=pltpu.VMEM)
SMEM = pl.BlockSpec(memory_space=pltpu.SMEM)
COST = pl.CostEstimate(flops=1, bytes_accessed=1, transcendentals=0)


def params():
    return pltpu.CompilerParams(vmem_limit_bytes=8 * 2**20)


def times_transposed(left, right):
    return lax.dot_general(left, right, (((1,), (1,)), ((), ())), preferred_element_type=jnp.float32)


TILE = 256


def product_kernel(count, block, *refs):
    units, rest, out = refs[:count], refs[count:-1], refs[-1]
    x = units[0][...] if count == 1 else jnp.concatenate([u[...] for u in units], axis=0)
    rows = block.shape[0]
    tile = min(rows, TILE)
    for t in range(rows // tile):
        cut = pl.ds(t * tile, tile)
        value = times_transposed(block[cut], x).T
        for r in rest:
            value = value + r[:, cut]
        out[:, cut] = value.astype(out.dtype)


def product(block, units, rest=(), kind=jnp.float32):
    angles = sum(u.shape[0] for u in units)
    return pl.pallas_call(
        functools.partial(product_kernel, len(units)),
        out_shape=jax.ShapeDtypeStruct((angles, block.shape[0]), kind),
        in_specs=[VMEM] * (1 + len(units) + len(rest)),
        out_specs=VMEM,
        compiler_params=params(),
        cost_estimate=COST,
    )(block, *units, *rest)


def first_kernel(s, side, sides, block, keep, leave, product):
    width = keep.shape[0]
    x = sides[0].T
    x = jnp.concatenate(
        [x[unit_place(s, h) * width : (unit_place(s, h) + 1) * width] for h in range(2)], axis=0
    )
    product[...] = times_transposed(x, block[...])
    own = pl.multiple_of(side[0] * width, width)
    other = pl.multiple_of((1 - side[0]) * width, width)
    leave[...] = product[pl.ds(own, width)].astype(jnp.bfloat16)
    keep[...] = product[pl.ds(other, width)]


def first_products(s, side, sides, block):
    rows = block.shape[0]
    width = sides.shape[2] // UNITS
    return pl.pallas_call(
        functools.partial(first_kernel, s),
        out_shape=(
            jax.ShapeDtypeStruct((width, rows), jnp.float32),
            jax.ShapeDtypeStruct((width, rows), jnp.bfloat16),
        ),
        in_specs=[SMEM, VMEM, VMEM],
        out_specs=(VMEM, VMEM),
        scratch_shapes=[pltpu.VMEM((2 * width, rows), jnp.float32)],
        compiler_params=params(),
        cost_estimate=COST,
    )(side, sides, block)


def turn_kernel(width, side, sides, out, turned):
    turned[...] = sides[0].T
    for s in range(STREAMS):
        own = pl.multiple_of(unit_place(s, side[0]) * width, width)
        out[0, s] = turned[pl.ds(own, width)]


def turned_sides(side, sides):
    steps, rows, angles = sides.shape
    width = angles // UNITS
    return pl.pallas_call(
        functools.partial(turn_kernel, width),
        grid=(steps - 1,),
        out_shape=jax.ShapeDtypeStruct((steps - 1, STREAMS, width, rows), jnp.bfloat16),
        in_specs=[SMEM, pl.BlockSpec((1, rows, angles), lambda i: (i + 1, 0, 0))],
        out_specs=pl.BlockSpec((1, STREAMS, width, rows), lambda i: (i, 0, 0, 0)),
        scratch_shapes=[pltpu.VMEM((angles, rows), jnp.bfloat16)],
        compiler_params=params(),
        cost_estimate=COST,
    )(side, sides)


def wide(value):
    return value.astype(jnp.float32)


def narrow(value):
    return value.astype(jnp.bfloat16)


def unit_place(s, h):
    return STREAMS * h + (h if s == 0 else 1 - h)


class Order:
    def __init__(self):
        self.last = None

    def run(self, work, *values):
        if self.last is not None:
            *values, _ = lax.optimization_barrier((*values, self.last))
        result = work(*values)
        self.last = result[0] if isinstance(result, (tuple, list)) else result
        return result

    def block(self, blocks, index):
        self.last = lax.optimization_barrier(self.run(lambda v: v[index], blocks))
        return self.last


def make_per_device(n_row, n_col):
    def trade(value, axis, step):
        size = n_row if axis == "row" else n_col
        return lax.ppermute(value, axis, [(i, i ^ step) for i in range(size)])

    def more_rounds(value, axis):
        size = n_row if axis == "row" else n_col
        step = 4
        while step < size:
            value = value + wide(trade(narrow(value), axis, step))
            step *= 2
        return value

    def per_device(factor_blocks, inverse_blocks, right_sides):
        steps_total, group_rows, angles = right_sides.shape
        last_step = steps_total - 1
        place = lax.axis_index("row")
        core = lax.axis_index("col") & 1
        side = (place & 1) ^ core
        side_ref = side.astype(jnp.int32).reshape(1)
        width = angles // UNITS
        exact = n_row == UNITS
        order = Order()
        solved = [[None] * STREAMS for _ in range(steps_total)]
        state = [dict() for _ in range(STREAMS)]
        sums = [None] * (steps_total + 1)
        factors = [None] * steps_total
        inverses = [None] * steps_total

        def load_factor(step):
            if step < steps_total:
                factors[step] = order.block(factor_blocks, pair_index(step, step - 1))

        def load_inverse(step):
            if step < steps_total:
                inverses[step] = order.block(inverse_blocks, step)

        def older(step, blocks):
            if step >= steps_total:
                return
            for j in blocks:
                block = order.block(factor_blocks, pair_index(step, j))
                units = [u for s in range(STREAMS) for u in solved[j][s]]

                rest = [] if sums[step] is None else [sums[step]]
                sums[step] = order.run(
                    lambda block, *v: product(block, v[: len(units)], v[len(units) :]), block, *units, *rest
                )

        def older_part(s, step, u):
            first = (2 * s + u) * width
            return [] if sums[step] is None else [sums[step][first : first + width]]

        def factor_other(s, step):
            st = state[s]
            leaving = order.run(
                lambda block, x, *rest: product(block, [x], rest, jnp.bfloat16),
                factors[step],
                solved[step - 1][s][1],
                *older_part(s, step, 1),
            )
            st["swap"] = trade(leaving, "col", 1)

        def factor_own(s, step):
            state[s]["sum"] = order.run(
                lambda block, x, *rest: product(block, [x], rest),
                factors[step],
                solved[step - 1][s][0],
                *older_part(s, step, 0),
            )

        def chip_sum(s):
            def work(value, arrived):
                value = value + wide(arrived)
                return narrow(value), value

            st = state[s]
            leaving, st["sum"] = order.run(work, st["sum"], st["swap"])
            st["flight"] = trade(leaving, "col", 2) if n_col > 2 else None

        def residual(s, step):
            def work(side_values, value, *arrived):
                for a in arrived:
                    value = more_rounds(value + wide(a), "col")
                return narrow(wide(side_values) - value)

            st = state[s]
            arrived = [] if st["flight"] is None else [st["flight"]]
            st["own"] = order.run(work, base[step - 1, s], st["sum"], *arrived)
            st["swap"] = trade(st["own"], "col", 1)

        def inverse_own(s, step):
            st = state[s]
            if exact and step == last_step:
                own, other = st["own"], st["swap"]
                stays = core == s
                st["own"], st["swap"] = jnp.where(stays, other, own), jnp.where(stays, own, other)
            leaving = order.run(
                lambda block, x: product(block, [x], kind=jnp.bfloat16), inverses[step], st["own"]
            )
            st["flight"] = trade(leaving, "row", 1)

        def inverse_other(s, step):
            st = state[s]
            st["total"] = order.run(lambda block, x: product(block, [x]), inverses[step], st["swap"])

        def pair_sum(s):
            def work(value, arrived):
                value = value + wide(arrived)
                return narrow(value), value

            st = state[s]
            st["leaving"], st["total"] = order.run(work, st["total"], st["flight"])

        def cross(s):
            st = state[s]
            st["flight"] = trade(st["leaving"], "row", 2) if n_row > 2 else None

        def final_cross(s):
            st = state[s]
            pairs = [(r ^ 2, r) for r in range(n_row) if r in [unit_place(s, h) for h in range(2)]]
            st["flight"] = lax.ppermute(st["leaving"], "row", pairs)

        def solve(s, step):
            def work(value, *arrived):
                for a in arrived:
                    value = more_rounds(value + wide(a), "row")
                return narrow(value)

            st = state[s]
            arrived = [] if st["flight"] is None else [st["flight"]]
            other = order.run(work, st["total"], *arrived)
            solved[step][s] = (trade(other, "row", 1), other)

        inverses[0] = order.block(inverse_blocks, 0)
        def first(s):
            state[s]["total"], leaving = order.run(
                lambda v, w: first_products(s, side_ref, v, w), right_sides, inverses[0]
            )
            state[s]["flight"] = trade(leaving, "row", 1)

        first(0)
        first(1)
        if steps_total > 1:
            base = order.run(lambda v: turned_sides(side_ref, v), right_sides)
        pair_sum(0)
        cross(0)
        load_factor(1)

        for step in range(1, steps_total):
            final = exact and step == last_step
            solve(0, step - 1)
            factor_other(0, step)
            pair_sum(1)
            cross(1)
            factor_own(0, step)
            chip_sum(0)
            older(step + 1, range(step - 1))
            load_factor(step + 1)
            load_inverse(step)
            if final:
                residual(0, step)
                solve(1, step - 1)
                factor_other(1, step)
                factor_own(1, step)
                chip_sum(1)
                inverse_own(0, step)
                inverse_other(0, step)
                residual(1, step)
                pair_sum(0)
                final_cross(0)
                inverse_own(1, step)
                inverse_other(1, step)
                continue
            solve(1, step - 1)
            factor_other(1, step)
            residual(0, step)
            inverse_own(0, step)
            factor_own(1, step)
            chip_sum(1)
            older(step + 1, [step - 1])
            inverse_other(0, step)
            pair_sum(0)
            cross(0)
            residual(1, step)
            inverse_own(1, step)
            inverse_other(1, step)
        pair_sum(1)

        outputs = []
        for step in range(steps_total):
            if exact and step == last_step:
                final_cross(1)
                first_gives = ((place ^ (place >> 1)) & 1) == 0
                found = jnp.where(first_gives, state[0]["total"], state[1]["total"])
                found = found + wide(jnp.where(first_gives, state[0]["flight"], state[1]["flight"]))
                found = narrow(found)
                outputs.append(found.T)
                continue
            if step == last_step:
                solve(0, step)
                cross(1)
                solve(1, step)
            unit = place * UNITS // n_row
            found = solved[step][0][0]
            for s in range(STREAMS):
                for u in range(2):
                    found = jnp.where(unit == unit_place(s, u ^ side), solved[step][s][u], found)
            if not exact:
                slot = angles // n_row
                found = lax.dynamic_slice_in_dim(found, (place * slot) % width, slot, 0)
            outputs.append(found.T)
        return jnp.stack(outputs, axis=0)

    return per_device


def solution(mesh):
    placed = (P("groups", "row", "col"), P("groups", "col", "row"), P("groups", "row", None))
    return jax.shard_map(
        make_per_device(mesh.shape["row"], mesh.shape["col"]),
        mesh=mesh,
        in_specs=placed,
        out_specs=P("groups", "col", "row"),
        check_vma=False,
    )
```

```python
import functools

import jax
import jax.numpy as jnp
from jax import lax
from jax.experimental import pallas as pl
from jax.experimental.pallas import tpu as pltpu
from jax.sharding import PartitionSpec as P

STREAMS = 2
UNITS = 2 * STREAMS


def pair_index(block_row, column_index):
    return block_row * (block_row - 1) // 2 + column_index


VMEM = pl.BlockSpec(memory_space=pltpu.VMEM)
SMEM = pl.BlockSpec(memory_space=pltpu.SMEM)
COST = pl.CostEstimate(flops=1, bytes_accessed=1, transcendentals=0)


def params():
    return pltpu.CompilerParams(vmem_limit_bytes=8 * 2**20)


def times_transposed(left, right):
    return lax.dot_general(left, right, (((1,), (1,)), ((), ())), preferred_element_type=jnp.float32)


TILE = 256


def product_kernel(count, block, *refs):
    units, rest, out = refs[:count], refs[count:-1], refs[-1]
    x = units[0][...] if count == 1 else jnp.concatenate([u[...] for u in units], axis=0)
    rows = block.shape[0]
    tile = min(rows, TILE)
    for t in range(rows // tile):
        cut = pl.ds(t * tile, tile)
        value = times_transposed(block[cut], x).T
        for r in rest:
            value = value + r[:, cut]
        out[:, cut] = value.astype(out.dtype)


def product(block, units, rest=(), kind=jnp.float32):
    angles = sum(u.shape[0] for u in units)
    return pl.pallas_call(
        functools.partial(product_kernel, len(units)),
        out_shape=jax.ShapeDtypeStruct((angles, block.shape[0]), kind),
        in_specs=[VMEM] * (1 + len(units) + len(rest)),
        out_specs=VMEM,
        compiler_params=params(),
        cost_estimate=COST,
    )(block, *units, *rest)


def first_kernel(s, side, right, block, keep, leave, product):
    width = keep.shape[0]
    x = right[...].T
    x = jnp.concatenate(
        [x[unit_place(s, h) * width : (unit_place(s, h) + 1) * width] for h in range(2)], axis=0
    )
    product[...] = times_transposed(x, block[...])
    own = pl.multiple_of(side[0] * width, width)
    other = pl.multiple_of((1 - side[0]) * width, width)
    leave[...] = product[pl.ds(own, width)].astype(jnp.bfloat16)
    keep[...] = product[pl.ds(other, width)]


def first_products(s, side, right, block):
    rows = block.shape[0]
    width = right.shape[1] // UNITS
    return pl.pallas_call(
        functools.partial(first_kernel, s),
        out_shape=(
            jax.ShapeDtypeStruct((width, rows), jnp.float32),
            jax.ShapeDtypeStruct((width, rows), jnp.bfloat16),
        ),
        in_specs=[SMEM, VMEM, VMEM],
        out_specs=(VMEM, VMEM),
        scratch_shapes=[pltpu.VMEM((2 * width, rows), jnp.float32)],
        compiler_params=params(),
        cost_estimate=COST,
    )(side, right, block)


def turn_kernel(width, side, sides, out, turned):
    turned[...] = sides[0].T
    for s in range(STREAMS):
        own = pl.multiple_of(unit_place(s, side[0]) * width, width)
        out[0, s] = turned[pl.ds(own, width)]


def turned_sides(side, sides):
    steps, rows, angles = sides.shape
    width = angles // UNITS
    return pl.pallas_call(
        functools.partial(turn_kernel, width),
        grid=(steps - 1,),
        out_shape=jax.ShapeDtypeStruct((steps - 1, STREAMS, width, rows), jnp.bfloat16),
        in_specs=[SMEM, pl.BlockSpec((1, rows, angles), lambda i: (i + 1, 0, 0))],
        out_specs=pl.BlockSpec((1, STREAMS, width, rows), lambda i: (i, 0, 0, 0)),
        scratch_shapes=[pltpu.VMEM((angles, rows), jnp.bfloat16)],
        compiler_params=params(),
        cost_estimate=COST,
    )(side, sides)


def wide(value):
    return value.astype(jnp.float32)


def narrow(value):
    return value.astype(jnp.bfloat16)


def unit_place(s, h):
    return STREAMS * h + (h if s == 0 else 1 - h)


class Order:
    def __init__(self):
        self.last = None

    def run(self, work, *values):
        if self.last is not None:
            *values, _ = lax.optimization_barrier((*values, self.last))
        result = work(*values)
        self.last = result[0] if isinstance(result, (tuple, list)) else result
        return result

    def block(self, blocks, index):
        self.last = lax.optimization_barrier(self.run(lambda v: v[index], blocks))
        return self.last


def make_per_device(n_row, n_col):
    def trade(value, axis, step):
        size = n_row if axis == "row" else n_col
        return lax.ppermute(value, axis, [(i, i ^ step) for i in range(size)])

    def more_rounds(value, axis):
        size = n_row if axis == "row" else n_col
        step = 4
        while step < size:
            value = value + wide(trade(narrow(value), axis, step))
            step *= 2
        return value

    def per_device(factor_blocks, inverse_blocks, right_sides):
        steps_total, group_rows, angles = right_sides.shape
        col_rows = inverse_blocks.shape[1]
        last_step = steps_total - 1
        place = lax.axis_index("row")
        core = lax.axis_index("col") & 1
        side = (place & 1) ^ core
        side_ref = side.astype(jnp.int32).reshape(1)
        width = angles // UNITS
        exact = n_row == UNITS
        order = Order()
        solved = [[None] * STREAMS for _ in range(steps_total)]
        state = [dict() for _ in range(STREAMS)]
        sums = [None] * (steps_total + 1)
        factors = [None] * steps_total
        inverses = [None] * steps_total

        def load_factor(step):
            if step < steps_total:
                factors[step] = order.block(factor_blocks, pair_index(step, step - 1))

        def load_inverse(step):
            if step < steps_total:
                inverses[step] = order.block(inverse_blocks, step)

        def older(step, blocks):
            if step >= steps_total:
                return
            for j in blocks:
                block = order.block(factor_blocks, pair_index(step, j))
                units = [u for s in range(STREAMS) for u in solved[j][s]]

                rest = [] if sums[step] is None else [sums[step]]
                sums[step] = order.run(
                    lambda block, *v: product(block, v[: len(units)], v[len(units) :]), block, *units, *rest
                )

        def older_part(s, step, u):
            first = (2 * s + u) * width
            return [] if sums[step] is None else [sums[step][first : first + width]]

        def factor_other(s, step):
            st = state[s]
            leaving = order.run(
                lambda block, x, *rest: product(block, [x], rest, jnp.bfloat16),
                factors[step],
                solved[step - 1][s][1],
                *older_part(s, step, 1),
            )
            st["swap"] = trade(leaving, "col", 1)

        def factor_own(s, step):
            state[s]["sum"] = order.run(
                lambda block, x, *rest: product(block, [x], rest),
                factors[step],
                solved[step - 1][s][0],
                *older_part(s, step, 0),
            )

        def chip_sum(s):
            def work(value, arrived):
                value = value + wide(arrived)
                return narrow(value), value

            st = state[s]
            leaving, st["sum"] = order.run(work, st["sum"], st["swap"])
            st["flight"] = trade(leaving, "col", 2) if n_col > 2 else None

        def residual(s, step):
            def work(side_values, value, *arrived):
                for a in arrived:
                    value = more_rounds(value + wide(a), "col")
                return narrow(wide(side_values) - value)

            st = state[s]
            arrived = [] if st["flight"] is None else [st["flight"]]
            st["own"] = order.run(work, base[step - 1, s], st["sum"], *arrived)
            st["swap"] = trade(st["own"], "col", 1)

        def trade_sums(value, step, keep=lambda z: True):
            pairs = []
            for z in range(n_row):
                for c in range(n_col):
                    first_place = z - z % step
                    if keep(z ^ step) and first_place * group_rows < (c + 1) * col_rows:
                        pairs.append((z * n_col + c, (z ^ step) * n_col + c))
            return lax.ppermute(value, ("row", "col"), pairs)

        def inverse_own(s, step):
            st = state[s]
            if exact and step == last_step:
                own, other = st["own"], st["swap"]
                stays = core == s
                st["own"], st["swap"] = jnp.where(stays, other, own), jnp.where(stays, own, other)
            leaving = order.run(
                lambda block, x: product(block, [x], kind=jnp.bfloat16), inverses[step], st["own"]
            )
            st["flight"] = trade_sums(leaving, 1)

        def inverse_other(s, step):
            st = state[s]
            st["total"] = order.run(lambda block, x: product(block, [x]), inverses[step], st["swap"])

        def pair_sum(s):
            def work(value, arrived):
                value = value + wide(arrived)
                return narrow(value), value

            st = state[s]
            st["leaving"], st["total"] = order.run(work, st["total"], st["flight"])

        def cross(s):
            st = state[s]
            st["flight"] = trade_sums(st["leaving"], 2) if n_row > 2 else None

        def final_cross(s):
            st = state[s]
            places = [unit_place(s, h) for h in range(2)]
            st["flight"] = trade_sums(st["leaving"], 2, lambda r: r in places)

        def solve(s, step):
            def work(value, *arrived):
                for a in arrived:
                    value = more_rounds(value + wide(a), "row")
                return narrow(value)

            st = state[s]
            arrived = [] if st["flight"] is None else [st["flight"]]
            other = order.run(work, st["total"], *arrived)
            solved[step][s] = (trade(other, "row", 1), other)

        inverses[0] = order.block(inverse_blocks, 0)
        right = order.block(right_sides, 0)
        def first(s):
            state[s]["total"], leaving = order.run(
                lambda v, w: first_products(s, side_ref, v, w), right, inverses[0]
            )
            state[s]["flight"] = trade_sums(leaving, 1)

        first(0)
        first(1)
        if steps_total > 1:
            base = order.run(lambda v: turned_sides(side_ref, v), right_sides)
        pair_sum(0)
        cross(0)
        load_factor(1)

        for step in range(1, steps_total):
            final = exact and step == last_step
            solve(0, step - 1)
            factor_other(0, step)
            pair_sum(1)
            cross(1)
            factor_own(0, step)
            chip_sum(0)
            older(step + 1, range(step - 1))
            load_factor(step + 1)
            load_inverse(step)
            if final:
                residual(0, step)
                solve(1, step - 1)
                factor_other(1, step)
                factor_own(1, step)
                chip_sum(1)
                inverse_own(0, step)
                inverse_other(0, step)
                residual(1, step)
                pair_sum(0)
                final_cross(0)
                inverse_own(1, step)
                inverse_other(1, step)
                continue
            solve(1, step - 1)
            factor_other(1, step)
            residual(0, step)
            inverse_own(0, step)
            factor_own(1, step)
            chip_sum(1)
            older(step + 1, [step - 1])
            inverse_other(0, step)
            pair_sum(0)
            cross(0)
            residual(1, step)
            inverse_own(1, step)
            inverse_other(1, step)
        pair_sum(1)

        outputs = []
        for step in range(steps_total):
            if exact and step == last_step:
                final_cross(1)
                first_gives = ((place ^ (place >> 1)) & 1) == 0
                found = jnp.where(first_gives, state[0]["total"], state[1]["total"])
                found = found + wide(jnp.where(first_gives, state[0]["flight"], state[1]["flight"]))
                found = narrow(found)
                outputs.append(found.T)
                continue
            if step == last_step:
                solve(0, step)
                cross(1)
                solve(1, step)
            unit = place * UNITS // n_row
            found = solved[step][0][0]
            for s in range(STREAMS):
                for u in range(2):
                    found = jnp.where(unit == unit_place(s, u ^ side), solved[step][s][u], found)
            if not exact:
                slot = angles // n_row
                found = lax.dynamic_slice_in_dim(found, (place * slot) % width, slot, 0)
            outputs.append(found.T)
        return jnp.stack(outputs, axis=0)

    return per_device


def solution(mesh):
    placed = (P("groups", "row", "col"), P("groups", "col", "row"), P("groups", "row", None))
    return jax.shard_map(
        make_per_device(mesh.shape["row"], mesh.shape["col"]),
        mesh=mesh,
        in_specs=placed,
        out_specs=P("groups", "col", "row"),
        check_vma=False,
    )
```

```python
import functools

import jax
import jax.numpy as jnp
from jax import lax
from jax.experimental import pallas as pl
from jax.experimental.pallas import tpu as pltpu
from jax.sharding import PartitionSpec as P

STREAMS = 2
UNITS = 2 * STREAMS


def pair_index(block_row, column_index):
    return block_row * (block_row - 1) // 2 + column_index


VMEM = pl.BlockSpec(memory_space=pltpu.VMEM)
SMEM = pl.BlockSpec(memory_space=pltpu.SMEM)
COST = pl.CostEstimate(flops=1, bytes_accessed=1, transcendentals=0)


def params():
    return pltpu.CompilerParams(vmem_limit_bytes=8 * 2**20)


def times_transposed(left, right):
    return lax.dot_general(left, right, (((1,), (1,)), ((), ())), preferred_element_type=jnp.float32)


TILE = 256


def product_kernel(count, block, *refs):
    units, rest, out = refs[:count], refs[count:-1], refs[-1]
    x = units[0][...] if count == 1 else jnp.concatenate([u[...] for u in units], axis=0)
    rows = block.shape[0]
    tile = min(rows, TILE)
    for t in range(rows // tile):
        cut = pl.ds(t * tile, tile)
        value = times_transposed(block[cut], x).T
        for r in rest:
            value = value + r[:, cut]
        out[:, cut] = value.astype(out.dtype)


def product(block, units, rest=(), kind=jnp.float32):
    angles = sum(u.shape[0] for u in units)
    return pl.pallas_call(
        functools.partial(product_kernel, len(units)),
        out_shape=jax.ShapeDtypeStruct((angles, block.shape[0]), kind),
        in_specs=[VMEM] * (1 + len(units) + len(rest)),
        out_specs=VMEM,
        compiler_params=params(),
        cost_estimate=COST,
    )(block, *units, *rest)


def first_kernel(s, side, right, block, keep, leave, product):
    width = keep.shape[0]
    x = right[...].T
    x = jnp.concatenate(
        [x[unit_place(s, h) * width : (unit_place(s, h) + 1) * width] for h in range(2)], axis=0
    )
    product[...] = times_transposed(x, block[...])
    own = pl.multiple_of(side[0] * width, width)
    other = pl.multiple_of((1 - side[0]) * width, width)
    leave[...] = product[pl.ds(own, width)].astype(jnp.bfloat16)
    keep[...] = product[pl.ds(other, width)]


def first_products(s, side, right, block):
    rows = block.shape[0]
    width = right.shape[1] // UNITS
    return pl.pallas_call(
        functools.partial(first_kernel, s),
        out_shape=(
            jax.ShapeDtypeStruct((width, rows), jnp.float32),
            jax.ShapeDtypeStruct((width, rows), jnp.bfloat16),
        ),
        in_specs=[SMEM, VMEM, VMEM],
        out_specs=(VMEM, VMEM),
        scratch_shapes=[pltpu.VMEM((2 * width, rows), jnp.float32)],
        compiler_params=params(),
        cost_estimate=COST,
    )(side, right, block)


def turn_kernel(width, side, sides, out, turned):
    turned[...] = sides[0].T
    for s in range(STREAMS):
        own = pl.multiple_of(unit_place(s, side[0]) * width, width)
        out[0, s] = turned[pl.ds(own, width)]


def turned_sides(side, sides):
    steps, rows, angles = sides.shape
    width = angles // UNITS
    return pl.pallas_call(
        functools.partial(turn_kernel, width),
        grid=(steps - 1,),
        out_shape=jax.ShapeDtypeStruct((steps - 1, STREAMS, width, rows), jnp.bfloat16),
        in_specs=[SMEM, pl.BlockSpec((1, rows, angles), lambda i: (i + 1, 0, 0))],
        out_specs=pl.BlockSpec((1, STREAMS, width, rows), lambda i: (i, 0, 0, 0)),
        scratch_shapes=[pltpu.VMEM((angles, rows), jnp.bfloat16)],
        compiler_params=params(),
        cost_estimate=COST,
    )(side, sides)


def wide(value):
    return value.astype(jnp.float32)


def narrow(value):
    return value.astype(jnp.bfloat16)


def unit_place(s, h):
    return STREAMS * h + (h if s == 0 else 1 - h)


class Order:
    def __init__(self):
        self.last = None

    def run(self, work, *values):
        if self.last is not None:
            *values, _ = lax.optimization_barrier((*values, self.last))
        result = work(*values)
        self.last = result[0] if isinstance(result, (tuple, list)) else result
        return result

    def block(self, blocks, index):
        self.last = lax.optimization_barrier(self.run(lambda v: v[index], blocks))
        return self.last


def make_per_device(n_row, n_col):
    def trade(value, axis, step):
        size = n_row if axis == "row" else n_col
        return lax.ppermute(value, axis, [(i, i ^ step) for i in range(size)])

    def more_rounds(value, axis):
        size = n_row if axis == "row" else n_col
        step = 4
        while step < size:
            value = value + wide(trade(narrow(value), axis, step))
            step *= 2
        return value

    def per_device(factor_blocks, inverse_blocks, right_sides):
        steps_total, group_rows, angles = right_sides.shape
        last_step = steps_total - 1
        place = lax.axis_index("row")
        core = lax.axis_index("col") & 1
        side = (place & 1) ^ core
        side_ref = side.astype(jnp.int32).reshape(1)
        width = angles // UNITS
        exact = n_row == UNITS
        order = Order()
        solved = [[None] * STREAMS for _ in range(steps_total)]
        state = [dict() for _ in range(STREAMS)]
        sums = [None] * (steps_total + 1)
        factors = [None] * steps_total
        inverses = [None] * steps_total

        def load_factor(step):
            if step < steps_total:
                factors[step] = order.block(factor_blocks, pair_index(step, step - 1))

        def load_inverse(step):
            if step < steps_total:
                inverses[step] = order.block(inverse_blocks, step)

        def older(step, blocks):
            if step >= steps_total:
                return
            for j in blocks:
                block = order.block(factor_blocks, pair_index(step, j))
                units = [u for s in range(STREAMS) for u in solved[j][s]]

                rest = [] if sums[step] is None else [sums[step]]
                sums[step] = order.run(
                    lambda block, *v: product(block, v[: len(units)], v[len(units) :]), block, *units, *rest
                )

        def older_part(s, step, u):
            first = (2 * s + u) * width
            return [] if sums[step] is None else [sums[step][first : first + width]]

        def factor_other(s, step):
            st = state[s]
            leaving = order.run(
                lambda block, x, *rest: product(block, [x], rest, jnp.bfloat16),
                factors[step],
                solved[step - 1][s][1],
                *older_part(s, step, 1),
            )
            st["swap"] = trade(leaving, "col", 1)

        def factor_own(s, step):
            state[s]["sum"] = order.run(
                lambda block, x, *rest: product(block, [x], rest),
                factors[step],
                solved[step - 1][s][0],
                *older_part(s, step, 0),
            )

        def chip_sum(s):
            def work(value, arrived):
                value = value + wide(arrived)
                return narrow(value), value

            st = state[s]
            leaving, st["sum"] = order.run(work, st["sum"], st["swap"])
            st["flight"] = trade(leaving, "col", 2) if n_col > 2 else None

        def residual(s, step):
            def work(side_values, value, *arrived):
                for a in arrived:
                    value = more_rounds(value + wide(a), "col")
                return narrow(wide(side_values) - value)

            st = state[s]
            arrived = [] if st["flight"] is None else [st["flight"]]
            st["own"] = order.run(work, base[step - 1, s], st["sum"], *arrived)
            st["swap"] = trade(st["own"], "col", 1)

        def inverse_own(s, step):
            st = state[s]
            if exact and step == last_step:
                own, other = st["own"], st["swap"]
                stays = core == s
                st["own"], st["swap"] = jnp.where(stays, other, own), jnp.where(stays, own, other)
            leaving = order.run(
                lambda block, x: product(block, [x], kind=jnp.bfloat16), inverses[step], st["own"]
            )
            st["flight"] = trade(leaving, "row", 1)

        def inverse_other(s, step):
            st = state[s]
            st["total"] = order.run(lambda block, x: product(block, [x]), inverses[step], st["swap"])

        def pair_sum(s):
            def work(value, arrived):
                value = value + wide(arrived)
                return narrow(value), value

            st = state[s]
            st["leaving"], st["total"] = order.run(work, st["total"], st["flight"])

        def cross(s):
            st = state[s]
            st["flight"] = trade(st["leaving"], "row", 2) if n_row > 2 else None

        def final_cross(s):
            st = state[s]
            pairs = [(r ^ 2, r) for r in range(n_row) if r in [unit_place(s, h) for h in range(2)]]
            st["flight"] = lax.ppermute(st["leaving"], "row", pairs)

        def solve(s, step):
            def work(value, *arrived):
                for a in arrived:
                    value = more_rounds(value + wide(a), "row")
                return narrow(value)

            st = state[s]
            arrived = [] if st["flight"] is None else [st["flight"]]
            other = order.run(work, st["total"], *arrived)
            solved[step][s] = (trade(other, "row", 1), other)

        inverses[0] = order.block(inverse_blocks, 0)
        right = order.block(right_sides, 0)
        def first(s):
            state[s]["total"], leaving = order.run(
                lambda v, w: first_products(s, side_ref, v, w), right, inverses[0]
            )
            state[s]["flight"] = trade(leaving, "row", 1)

        first(0)
        first(1)
        if steps_total > 1:
            base = order.run(lambda v: turned_sides(side_ref, v), right_sides)
        pair_sum(0)
        cross(0)
        load_factor(1)
        load_inverse(1)

        for step in range(1, steps_total):
            final = exact and step == last_step
            solve(0, step - 1)
            factor_other(0, step)
            pair_sum(1)
            cross(1)
            factor_own(0, step)
            chip_sum(0)
            older(step + 1, range(step - 1))
            load_factor(step + 1)
            if step > 1:
                load_inverse(step)
            if final:
                residual(0, step)
                solve(1, step - 1)
                factor_other(1, step)
                factor_own(1, step)
                chip_sum(1)
                inverse_own(0, step)
                inverse_other(0, step)
                residual(1, step)
                pair_sum(0)
                final_cross(0)
                inverse_own(1, step)
                inverse_other(1, step)
                continue
            solve(1, step - 1)
            factor_other(1, step)
            residual(0, step)
            inverse_own(0, step)
            factor_own(1, step)
            chip_sum(1)
            older(step + 1, [step - 1])
            inverse_other(0, step)
            pair_sum(0)
            cross(0)
            residual(1, step)
            inverse_own(1, step)
            inverse_other(1, step)
        pair_sum(1)

        outputs = []
        for step in range(steps_total):
            if exact and step == last_step:
                final_cross(1)
                first_gives = ((place ^ (place >> 1)) & 1) == 0
                found = jnp.where(first_gives, state[0]["total"], state[1]["total"])
                found = found + wide(jnp.where(first_gives, state[0]["flight"], state[1]["flight"]))
                found = narrow(found)
                outputs.append(found.T)
                continue
            if step == last_step:
                solve(0, step)
                cross(1)
                solve(1, step)
            unit = place * UNITS // n_row
            found = solved[step][0][0]
            for s in range(STREAMS):
                for u in range(2):
                    found = jnp.where(unit == unit_place(s, u ^ side), solved[step][s][u], found)
            if not exact:
                slot = angles // n_row
                found = lax.dynamic_slice_in_dim(found, (place * slot) % width, slot, 0)
            outputs.append(found.T)
        return jnp.stack(outputs, axis=0)

    return per_device


def solution(mesh):
    placed = (P("groups", "row", "col"), P("groups", "col", "row"), P("groups", "row", None))
    return jax.shard_map(
        make_per_device(mesh.shape["row"], mesh.shape["col"]),
        mesh=mesh,
        in_specs=placed,
        out_specs=P("groups", "col", "row"),
        check_vma=False,
    )
```
